256 devices in a mesh: section: 32 (over x, y, core), dp: 8 (over z).
Axes of the slice: x: 4, y: 4, z: 8, core: 2. Of those that a mesh axis runs over, the one named last changes fastest.
Arguments:
- inputs: bfloat16 [8, 128, 2560], P('dp'), may hold values from -6 to 6
- span_lengths: int32 [8, 8], P('dp'), may hold values from 1 to 20, 128 in all within a row
- qkv_weight: bfloat16 [32, 2560, 3840], P('section', 'dp'), may hold values from -0.125 to 0.125
- out_weight: bfloat16 [32, 2560, 1280], P('section', 'dp'), may hold values from -0.25 to 0.25
Outputs:
- hidden_out: bfloat16 [8, 128, 2560], P('dp', 'section')
The draws below stay inside these ranges and needn't reach their ends.
Inputs may be any that keep to these rules, and one draw needn't show every extreme that they name: `span_lengths`: each row sums to 128, and its largest entry is exactly 20.
All inputs are finite; a program needn't handle non-finite values.
Results may differ from the reference program's by a relative error of at most 0.027.
Values may be sent and summed in bfloat16 or wider, within the bound.
A program may use at most 128 MiB of HBM per device.

```python
import math
import jax
import jax.numpy as jnp
import numpy as np
from jax import lax

DW = 2560
HD = 128
HEADS = 40
GROUP = 4
SPANS = 8
LEN = 128
CMAX = 20
HEADS_DEV = 10
LAYERS = 8
SEQS = 8
N_SECTION = 32


def levels(own_key, shape, shards, low, high):
    def one(axis_at, blocks):
        heights = jax.random.uniform(jax.random.fold_in(jax.random.fold_in(own_key, 6), axis_at), (blocks,), jnp.float32, low / len(shards), high / len(shards))
        return jnp.repeat(jnp.exp(heights), shape[axis_at] // blocks).reshape((-1,) + (1,) * (len(shape) - axis_at - 1))

    factor_of = one(*shards[0])
    for cut in shards[1:]:
        factor_of = factor_of * one(*cut)
    return factor_of


def length_profile(amount, total, limit, slope):
    loads = [(1 << 20) // math.isqrt(standing ** slope) + 1 for standing in range(2, amount + 1)]
    rest, counts = total - limit - (amount - 1), [1] * (amount - 1)
    while rest > 0:
        free = [i for i in range(amount - 1) if counts[i] < limit]
        pool, remaining = sum([loads[i] for i in free]), rest
        for i in free:
            extra = min(limit - counts[i], max(1, remaining * loads[i] // pool), rest)
            counts[i] = counts[i] + extra
            rest = rest - extra
    return np.array([limit] + counts)


def uneven_parts(rng, amount, total, most, lean):
    if amount == 2:
        one = jax.random.randint(rng, (), max(1, total - most), min(most, total - 1) + 1)
        return jnp.stack([one, total - one])
    tallies = jnp.asarray(length_profile(amount, total, most, lean), jnp.int32)
    pairs = (amount - 1) // 2
    donor, sink = tallies[1:1 + 2 * pairs:2], tallies[2:2 + 2 * pairs:2]
    slack = jnp.minimum(donor - 1, most - sink)
    shifted = jax.random.randint(jax.random.fold_in(rng, 1), (pairs,), 0, 1 << 20) % (slack + 1)
    tallies = tallies.at[1:1 + 2 * pairs:2].set(donor - shifted).at[2:2 + 2 * pairs:2].set(sink + shifted)
    return tallies[jax.random.permutation(jax.random.fold_in(rng, 2), amount)]


def gaussian(own_key, dims, spread, most, split=(), kind=jnp.bfloat16):
    entries = jax.random.normal(own_key, dims, jnp.float32) * spread
    if len(split) > 0:
        entries = levels(own_key, dims, split, -0.22, 0.18) * entries
    return jnp.clip(entries, min=-most, max=most).astype(kind)


def setup_inputs(seed: int = 0) -> dict:
    key_list = jax.random.split(jax.random.key(seed), 5)
    inputs = gaussian(key_list[0], (SEQS, LEN, DW), 1.0, 6.0, ((0, 8),))
    span_lengths = jax.vmap(lambda own: uneven_parts(own, SPANS, LEN, CMAX, 2))(jax.random.split(key_list[1], SEQS)).reshape((SEQS, SPANS)).astype(jnp.int32)
    qkv_weight = gaussian(key_list[2], (N_SECTION, DW, 3 * HEADS_DEV * HD), DW ** -0.5, 0.125, ((0, 32), (1, 8)))
    out_weight = gaussian(key_list[3], (N_SECTION, DW, HEADS_DEV * HD), (HEADS * HD // 8) ** -0.5, 0.25, ((0, 32), (1, 8)))
    return {"inputs": inputs, "span_lengths": span_lengths, "qkv_weight": qkv_weight, "out_weight": out_weight}


def layer_norm(hidden):
    values = hidden.astype(jnp.float32)
    row_mean = lax.optimization_barrier(jnp.mean(values, axis=-1, keepdims=True))
    centred = values - row_mean
    row_var = lax.optimization_barrier(jnp.mean(centred * centred, axis=-1, keepdims=True))
    return (centred * lax.rsqrt(row_var + 1e-05)).astype(jnp.bfloat16)

def one_sequence(hidden, seg_lengths, qkv_weight, out_weight):
    head_cols = HEADS_DEV * HD
    seg_ends = jnp.cumsum(seg_lengths).astype(jnp.int32)
    seg_starts = (seg_ends - seg_lengths).astype(jnp.int32)
    positions = jnp.arange(LEN, dtype=jnp.int32)
    seg_of = lax.optimization_barrier(jnp.sum((seg_ends[None, :] <= positions[:, None]).astype(jnp.int32), axis=1, dtype=jnp.int32))
    previous = jnp.maximum(seg_of - 1, 0)
    seg_ids = jnp.arange(SPANS, dtype=jnp.int32)
    key_start = lax.optimization_barrier(jnp.sum(jnp.where(seg_ids[None, :] == previous[:, None], seg_starts[None, :], 0), axis=1, dtype=jnp.int32))
    allowed = (positions[None, :] >= key_start[:, None]) & (positions[None, :] <= positions[:, None])
    scale = HD ** (-0.5)
    for layer_index in range(LAYERS):
        normed = layer_norm(hidden)
        block_qkv = qkv_weight[layer_index * GROUP:(layer_index + 1) * GROUP].astype(jnp.float32)
        block_out = out_weight[layer_index * GROUP:(layer_index + 1) * GROUP].astype(jnp.float32)
        projected = jnp.einsum('sd,gdc->gsc', normed.astype(jnp.float32), block_qkv).astype(jnp.bfloat16)
        queries = projected[:, :, :head_cols].reshape(GROUP, LEN, HEADS_DEV, HD).astype(jnp.float32)
        keys = projected[:, :, head_cols:2 * head_cols].reshape(GROUP, LEN, HEADS_DEV, HD).astype(jnp.float32)
        values = projected[:, :, 2 * head_cols:].reshape(GROUP, LEN, HEADS_DEV, HD).astype(jnp.float32)
        scores = jnp.einsum('gqhe,gkhe->ghqk', queries, keys) * scale
        weights = jnp.where(allowed, jnp.exp(scores), 0.0)
        probs = (weights / lax.optimization_barrier(jnp.sum(weights, axis=-1, keepdims=True))).astype(jnp.bfloat16)
        attended = jnp.einsum('ghqk,gkhe->gqhe', probs.astype(jnp.float32), values).astype(jnp.bfloat16)
        attended = attended.reshape(GROUP, LEN, head_cols)
        update = jnp.einsum('gqc,gdc->qd', attended.astype(jnp.float32), block_out)
        hidden = (hidden.astype(jnp.float32) + update).astype(jnp.bfloat16)
    return hidden

def reference(inputs, span_lengths, qkv_weight, out_weight):
    return jax.vmap(one_sequence, in_axes=(0, 0, None, None))(inputs, span_lengths, qkv_weight, out_weight)
```

```python
import jax
import jax.numpy as jnp
from jax import lax
from jax.experimental import pallas as pl
from jax.experimental.pallas import tpu as pltpu
from jax.sharding import PartitionSpec as P

HD = 128
GROUP = 4
SPANS = 8
LEN = 128
DP = 8
WIDTH = 2560
ROWS = 320
SLOTS = 5
CHUNK = 16
CHUNKS = LEN // CHUNK
BACK = 48
KEYS = BACK + CHUNK
PIECE = 640
MESH = pl.DeviceIdType.MESH


def kernel(
    x_ref, ks_ref, qkv_ref, ow_ref, out_ref,
    w, hbuf, normed, kc, vc, ksb, part, sendb, rbuf, hnew, outb,
    sem_w, sem_z, sem_x, sem_y, sem_yx, sem_c, sem_c2, sem_cx,
    snd_y, snd_yx, snd_c, snd_c2, snd_cx,
    sem_k, snd_k, sem_h, snd_i, sem_r, snd_r, snd_h, sem_o,
):
    sec = lax.axis_index("section")
    z = lax.axis_index("dp")
    layers = lax.axis_size("section") // GROUP
    layer = sec // GROUP
    g = sec % GROUP
    base = layer * GROUP
    y_mate = base + (g + 2) % GROUP
    slot_y = (g + 2) % GROUP
    core = g % 2
    mate = g + 1 - 2 * core
    c_mate = base + mate
    slot_cy = (mate + 2) % GROUP
    zg = z % GROUP
    own_seq = z // 2 == g

    def remote(src, dst, s_sem, r_sem, to_sec, to_z):
        return pltpu.make_async_remote_copy(
            src_ref=src, dst_ref=dst, send_sem=s_sem, recv_sem=r_sem,
            device_id=(to_sec, to_z), device_id_type=MESH,
        )

    def drain(ref, sem):
        pltpu.make_async_copy(ref, ref, sem).wait()

    @pl.when(own_seq)
    def _():
        e = z % 2
        pltpu.make_async_copy(ks_ref, ksb.at[e], sem_k).start()
        for d in range(1, DP):
            remote(ks_ref, ksb.at[e], snd_k.at[d - 1], sem_k, sec, (z + d) % DP).start()

    feeds = own_seq & (layer == 0)

    def feed(c):
        e = z % 2
        src = x_ref.at[0, pl.ds(pl.multiple_of(c * CHUNK, CHUNK), CHUNK), :]
        dst = hbuf.at[c, pl.ds(pl.multiple_of(e * CHUNK, CHUNK), CHUNK), :]
        pltpu.make_async_copy(src, dst, sem_h.at[c]).start()
        for d in range(1, DP):
            remote(src, dst, snd_i.at[c], sem_h.at[c], sec, (z + d) % DP).start()

    @pl.when(feeds)
    def _():
        feed(0)

    def parts(i, slot):
        rows = pl.ds(pl.multiple_of(z * ROWS, ROWS), ROWS)
        col = lambda n: pl.ds(pl.multiple_of(n * HD, HD), HD)
        out = []
        for p in range(3):
            out.append((qkv_ref.at[0, :, col(10 * p + i)], w.at[slot, rows, pl.ds(HD * p, HD)]))
        out.append((ow_ref.at[0, :, col(i)], w.at[slot, rows, pl.ds(3 * HD, HD)]))
        return out

    def send_head(i, to_z, slot, d, s_sem, r_sem):
        @pl.when(to_z == z)
        def _():
            for src, dst in parts(i, slot):
                pltpu.make_async_copy(src, dst, r_sem.at[0]).start()

        @pl.when(to_z != z)
        def _():
            for src, dst in parts(i, slot):
                remote(src, dst, s_sem, r_sem.at[d], sec, to_z).start()

    def spread(n, _):
        k = lax.rem(n, 2)
        d = (1 - 2 * k) * ((n + 1) // 2)
        d = (d + DP) % DP
        to_z = (z + d) % DP
        send_head(to_z, to_z, g, d, sem_w.at[n], sem_z)

        @pl.when((to_z == g) | (to_z == g + GROUP))
        def _():
            m = to_z // GROUP
            send_head(8 + m, to_z, 4, d, sem_w.at[DP + m], sem_x)

        return 0

    lax.fori_loop(0, DP, spread, 0)

    def block(slot, d):
        return w.at[slot, pl.ds(pl.multiple_of((z + DP - d) % DP * ROWS, ROWS), ROWS), :]

    def order(n):
        k = lax.rem(n, 2)
        return ((1 - 2 * k) * ((n + 1) // 2) + DP) % DP

    def relay(n, _):
        @pl.when(n < DP)
        def _():
            d = order(n)
            drain(block(g, d), sem_z.at[d])
            b = block(g, d)
            remote(b, b, snd_y.at[d], sem_y.at[d], y_mate, z).start()
            remote(b, b, snd_c.at[d], sem_c.at[d], c_mate, z).start()

            @pl.when(zg == g)
            def _():
                x = block(4, d)
                drain(x, sem_x.at[d])
                remote(x, x, snd_yx.at[d], sem_yx.at[d], y_mate, z).start()
                remote(x, x, snd_cx.at[d], sem_cx.at[d], c_mate, z).start()

        @pl.when(n > 0)
        def _():
            d = order(n - 1)
            b = block(slot_y, d)
            drain(b, sem_y.at[d])
            remote(b, b, snd_c2.at[d], sem_c2.at[d], c_mate, z).start()

            @pl.when(zg == slot_y)
            def _():
                x = block(4, d)
                drain(x, sem_yx.at[d])
                remote(x, x, snd_cx.at[d], sem_cx.at[d], c_mate, z).start()

        return 0

    lax.fori_loop(0, DP + 1, relay, 0)

    kc[:, pl.ds(0, BACK), :] = jnp.zeros((2, BACK, SLOTS * HD), jnp.bfloat16)
    vc[:, pl.ds(0, BACK), :] = jnp.zeros((2, BACK, SLOTS * HD), jnp.bfloat16)

    def arrive(n, _):
        d = order(n)
        drain(block(mate, d), sem_c.at[d])
        drain(block(slot_cy, d), sem_c2.at[d])

        @pl.when((zg == mate) | (zg == slot_cy))
        def _():
            drain(block(4, d), sem_cx.at[d])

        return 0

    lax.fori_loop(0, DP, arrive, 0)
    drain(ksb, sem_k)

    e_own = z // GROUP
    cc_own = z % GROUP
    row_own = pl.ds(pl.multiple_of(e_own * CHUNK, CHUNK), CHUNK)
    col_own = pl.ds(pl.multiple_of(cc_own * PIECE, PIECE), PIECE)
    scale = HD ** (-0.5)
    last = layer == layers - 1

    def step(c, _):
        @pl.when(feeds & (c < CHUNKS - 1))
        def _():
            feed(c + 1)

        drain(hbuf.at[c], sem_h.at[c])
        values = hbuf[c].astype(jnp.float32)
        mean = jnp.mean(values, axis=-1, keepdims=True)
        centred = values - mean
        var = jnp.mean(centred * centred, axis=-1, keepdims=True)
        normed[...] = (centred * lax.rsqrt(var + 1e-05)).astype(jnp.bfloat16)

        def project(cols):
            mat = [w[s, :, pl.ds(p * HD, HD * n)] for s, p, n in cols]
            mat = mat[0] if len(mat) == 1 else jnp.concatenate(mat, axis=1)
            return jnp.dot(normed[...], mat, preferred_element_type=jnp.float32).astype(jnp.bfloat16)

        new = pl.ds(pl.multiple_of(c * CHUNK + BACK, CHUNK), CHUNK)
        queries = []
        for s in range(SLOTS):
            qk = project([(s, 0, 2)])
            queries.append(qk[:, :HD])
            kc[0, new, pl.ds(s * HD, HD)] = qk[:CHUNK, HD:]
            kc[1, new, pl.ds(s * HD, HD)] = qk[CHUNK:, HD:]
        for s in (0, 2, 4):
            n = 2 if s < 4 else 1
            v = project([(s + i, 2, 1) for i in range(n)])
            vc[0, new, pl.ds(s * HD, n * HD)] = v[:CHUNK]
            vc[1, new, pl.ds(s * HD, n * HD)] = v[CHUNK:]

        tok = pl.ds(pl.multiple_of(c * CHUNK, CHUNK), CHUNK)
        first = jnp.concatenate([ksb[0, tok, :], ksb[1, tok, :]], axis=0).astype(jnp.float32)
        row = lax.broadcasted_iota(jnp.int32, (2 * CHUNK, 2 * KEYS), 0)
        col = lax.broadcasted_iota(jnp.int32, (2 * CHUNK, 2 * KEYS), 1)
        same = (row < CHUNK) == (col < KEYS)
        key_pos = c * CHUNK - BACK + jnp.where(col < KEYS, col, col - KEYS)
        tok_pos = c * CHUNK + jnp.where(row < CHUNK, row, row - CHUNK)
        allowed = same & (key_pos <= tok_pos) & (key_pos.astype(jnp.float32) >= first)

        window = pl.ds(pl.multiple_of(c * CHUNK, CHUNK), KEYS)
        attended = []
        for s in range(SLOTS):
            cols = pl.ds(s * HD, HD)
            keys = jnp.concatenate([kc[0, window, cols], kc[1, window, cols]], axis=0)
            vals = jnp.concatenate([vc[0, window, cols], vc[1, window, cols]], axis=0)
            scores = lax.dot_general(
                queries[s], keys, (((1,), (1,)), ((), ())), preferred_element_type=jnp.float32
            ) * scale
            weights = jnp.where(allowed, jnp.exp(scores), 0.0)
            probs = (weights / jnp.sum(weights, axis=-1, keepdims=True)).astype(jnp.bfloat16)
            attended.append(
                jnp.dot(probs, vals, preferred_element_type=jnp.float32).astype(jnp.bfloat16)
            )

        for cc in range(GROUP):
            total = None
            rows = pl.ds(cc * PIECE, PIECE)
            for s in (0, 2, 4):
                n = 2 if s < 4 else 1
                lhs = attended[s] if n == 1 else jnp.concatenate(attended[s : s + n], axis=1)
                rhs = [w[s + i, rows, pl.ds(3 * HD, HD)] for i in range(n)]
                rhs = rhs[0] if n == 1 else jnp.concatenate(rhs, axis=1)
                term = lax.dot_general(
                    lhs, rhs, (((1,), (1,)), ((), ())), preferred_element_type=jnp.float32
                )
                total = term if total is None else total + term
            cols = pl.ds(cc * PIECE, PIECE)
            part[:, cols] = total
            sendb[c, :, cols] = total.astype(jnp.bfloat16)
            for e in range(2):
                to_z = e * GROUP + cc

                @pl.when(z != to_z)
                def _():
                    d = (to_z - z + DP) % DP
                    remote(
                        sendb.at[c, pl.ds(e * CHUNK, CHUNK), cols], rbuf.at[c, d - 1],
                        snd_r.at[c], sem_r.at[c], sec, to_z,
                    ).start()

        total = part[row_own, col_own] + hbuf[c, row_own, col_own].astype(jnp.float32)
        drain(rbuf.at[c], sem_r.at[c])
        for d in range(DP - 1):
            total = total + rbuf[c, d].astype(jnp.float32)
        hnew[c] = total.astype(jnp.bfloat16)

        @pl.when(jnp.logical_not(last))
        def _():
            for n in range(DP):
                to_z = (z + n) % DP
                remote(
                    hnew.at[c], hbuf.at[c, row_own, col_own],
                    snd_h.at[c], sem_h.at[c], sec + GROUP, to_z,
                ).start()

        @pl.when(last)
        def _():
            for k in range(GROUP):
                to_sec = c * GROUP + k
                to_z = 2 * g + e_own
                here = (to_sec == sec) & (to_z == z)

                @pl.when(here)
                def _():
                    pltpu.make_async_copy(hnew.at[c], outb.at[:, col_own], sem_o).start()

                @pl.when(jnp.logical_not(here))
                def _():
                    remote(
                        hnew.at[c], outb.at[:, col_own], snd_h.at[c], sem_o, to_sec, to_z
                    ).start()

        return 0

    lax.fori_loop(0, CHUNKS, step, 0)

    drain(outb, sem_o)
    out_ref[...] = outb[...]

    def sent(c, _):
        drain(rbuf.at[c], snd_r.at[c])

        @pl.when(jnp.logical_not(last))
        def _():
            drain(hbuf.at[c], snd_h.at[c])

        @pl.when(last)
        def _():
            own = (c == CHUNKS - 1) & (z == 2 * g + e_own)

            @pl.when(own)
            def _():
                drain(outb.at[:, pl.ds(0, 3 * PIECE)], snd_h.at[c])

            @pl.when(jnp.logical_not(own))
            def _():
                drain(outb, snd_h.at[c])

        @pl.when(feeds)
        def _():
            drain(x_ref.at[0, pl.ds(0, LEN - CHUNK), :], snd_i.at[c])

        d = c
        drain(block(g, d), snd_y.at[d])
        drain(block(g, d), snd_c.at[d])
        drain(block(slot_y, d), snd_c2.at[d])

        @pl.when(zg == g)
        def _():
            drain(block(4, d), snd_yx.at[d])

        @pl.when((zg == g) | (zg == slot_y))
        def _():
            drain(block(4, d), snd_cx.at[d])

        @pl.when(d > 0)
        def _():
            drain(block(g, 0), sem_w.at[d])

        return 0

    lax.fori_loop(0, CHUNKS, sent, 0)
    for m in range(2):
        @pl.when(z != g + GROUP * m)
        def _():
            drain(block(g, 0), sem_w.at[DP + m])

    @pl.when(own_seq)
    def _():
        for d in range(1, DP):
            drain(ks_ref, snd_k.at[d - 1])


def shards(inputs, span_lengths, qkv_weight, out_weight):
    sections = lax.axis_size("section")
    lengths = span_lengths[0]
    ends = jnp.cumsum(lengths)
    starts = ends - lengths
    pos = jnp.arange(LEN, dtype=jnp.int32)
    seg = jnp.sum((ends[None, :] <= pos[:, None]).astype(jnp.int32), axis=1)
    prev = jnp.maximum(seg - 1, 0)
    ids = jnp.arange(SPANS, dtype=jnp.int32)
    key_start = jnp.sum(jnp.where(ids[None, :] == prev[:, None], starts[None, :], 0), axis=1)
    key_start = jnp.broadcast_to(key_start.astype(jnp.bfloat16)[:, None], (LEN, HD))

    bf16 = jnp.bfloat16
    dma = lambda *n: pltpu.SemaphoreType.DMA(n)
    out = pl.pallas_call(
        kernel,
        out_shape=jax.ShapeDtypeStruct((CHUNK, WIDTH), bf16),
        in_specs=[pl.BlockSpec(memory_space=pl.ANY)] * 4,
        out_specs=pl.BlockSpec(memory_space=pltpu.VMEM),
        scratch_shapes=[
            pltpu.VMEM((SLOTS, WIDTH, 4 * HD), bf16),
            pltpu.VMEM((CHUNKS, 2 * CHUNK, WIDTH), bf16),
            pltpu.VMEM((2 * CHUNK, WIDTH), bf16),
            pltpu.VMEM((2, LEN + BACK, SLOTS * HD), bf16),
            pltpu.VMEM((2, LEN + BACK, SLOTS * HD), bf16),
            pltpu.VMEM((2, LEN, HD), bf16),
            pltpu.VMEM((2 * CHUNK, WIDTH), jnp.float32),
            pltpu.VMEM((CHUNKS, 2 * CHUNK, WIDTH), bf16),
            pltpu.VMEM((CHUNKS, DP - 1, CHUNK, PIECE), bf16),
            pltpu.VMEM((CHUNKS, CHUNK, PIECE), bf16),
            pltpu.VMEM((CHUNK, WIDTH), bf16),
            dma(DP + 2), dma(DP), dma(DP), dma(DP), dma(DP), dma(DP), dma(DP), dma(DP),
            dma(DP), dma(DP), dma(DP), dma(DP), dma(DP),
            pltpu.SemaphoreType.DMA, dma(DP - 1), dma(CHUNKS), dma(CHUNKS), dma(CHUNKS),
            dma(CHUNKS), dma(CHUNKS), pltpu.SemaphoreType.DMA,
        ],
        compiler_params=pltpu.CompilerParams(
            has_side_effects=True, vmem_limit_bytes=44 * 1024 * 1024
        ),
    )(inputs, key_start, qkv_weight, out_weight)
    rows = LEN // sections
    first = lax.axis_index("section") % (CHUNK // rows) * rows
    return lax.dynamic_slice(out, (first, 0), (rows, WIDTH))[None]


def solution(mesh):
    in_specs = (
        P("dp", None, None),
        P("dp", None),
        P("section", "dp", None),
        P("section", "dp", None),
    )
    out_specs = P("dp", "section", None)
    return jax.shard_map(shards, mesh=mesh, in_specs=in_specs, out_specs=out_specs, check_vma=False)
```

```python
import jax
import jax.numpy as jnp
from jax import lax
from jax.experimental import pallas as pl
from jax.experimental.pallas import tpu as pltpu
from jax.sharding import PartitionSpec as P

HD = 128
GROUP = 4
SPANS = 8
LEN = 128
DP = 8
WIDTH = 2560
ROWS = 320
SLOTS = 5
CHUNK = 16
CHUNKS = LEN // CHUNK
BACK = 48
KEYS = BACK + CHUNK
PIECE = 640
AHEAD = 2
MESH = pl.DeviceIdType.MESH


def kernel(
    x_ref, sp_ref, qkv_ref, ow_ref, out_ref,
    w, hbuf, normed, qbuf, kc, vc, span, first_ref, part, sendb, rbuf, hnew, outb,
    sem_w, sem_z, sem_x, sem_y, sem_yx, sem_c, sem_c2, sem_cx,
    snd_y, snd_yx, snd_c, snd_c2, snd_cx, snd_cx2,
    sem_k, snd_k, sem_h, snd_i, sem_r, snd_r, snd_h, sem_o,
):
    sec = lax.axis_index("section")
    z = lax.axis_index("dp")
    sections = lax.axis_size("section")
    layers = sections // GROUP
    layer = sec // GROUP
    last = layer == layers - 1
    g = sec % GROUP
    base = layer * GROUP
    slot_y = (g + 2) % GROUP
    y_mate = base + slot_y
    mate = g + 1 - 2 * (g % 2)
    c_mate = base + mate
    slot_cy = (mate + 2) % GROUP
    zg = z % GROUP

    q = (g + 2 * (layer % 2)) % GROUP
    q_z = (z % 2) * 2 + z % GROUP // 2
    e_z = z // GROUP
    own_seq = q_z == q
    e_own = z // GROUP
    cc_own = z % GROUP
    out_z = GROUP * e_own + 2 * (q % 2) + q // 2
    is_out = out_z == z

    def remote(src, dst, s_sem, r_sem, to_sec, to_z):
        return pltpu.make_async_remote_copy(
            src_ref=src, dst_ref=dst, send_sem=s_sem, recv_sem=r_sem,
            device_id=(to_sec, to_z), device_id_type=MESH,
        )

    def drain(ref, sem):
        pltpu.make_async_copy(ref, ref, sem).wait()

    barrier = pltpu.get_barrier_semaphore()

    def greet(to_sec, to_z):
        pl.semaphore_signal(barrier, inc=1, device_id=(to_sec, to_z), device_id_type=MESH)

    for d in range(1, DP):
        greet(sec, (z + d) % DP)
    greet(y_mate, z)
    greet(c_mate, z)
    for d in range(1, DP):
        greet(y_mate, (z + d) % DP)

    @pl.when(layer > 0)
    def _():
        for d in range(DP):
            greet(base - GROUP + slot_y, (z + d) % DP)

    g_out = (q_z + 2 * ((layers - 1) % 2)) % GROUP
    for cc in range(GROUP):
        from_sec, from_z = sections - GROUP + g_out, e_z * GROUP + cc

        @pl.when((from_sec != sec) | (from_z != z))
        def _():
            greet(from_sec, from_z)

    kc[:, pl.ds(0, BACK), :] = jnp.zeros((2, BACK, SLOTS * HD), jnp.bfloat16)
    vc[:, pl.ds(0, BACK), :] = jnp.zeros((2, BACK, SLOTS * HD), jnp.bfloat16)
    span[2] = jnp.zeros((8, HD), jnp.int32)
    span[2, pl.ds(0, 1), pl.ds(0, SPANS)] = sp_ref[...]

    @pl.when(jnp.logical_not(last))
    def _():
        pl.semaphore_wait(barrier, 2 * DP + DP)

    @pl.when(last & is_out)
    def _():
        pl.semaphore_wait(barrier, 2 * DP + sections - 1)

    @pl.when(last & jnp.logical_not(is_out))
    def _():
        pl.semaphore_wait(barrier, 2 * DP + sections)

    @pl.when(own_seq)
    def _():
        pltpu.make_async_copy(span.at[2], span.at[e_z], sem_k).start()
        for d in range(1, DP):
            remote(span.at[2], span.at[e_z], snd_k.at[d - 1], sem_k, sec, (z + d) % DP).start()

    feeds = own_seq & (layer == 0)

    def feed(c):
        src = x_ref.at[0, pl.ds(pl.multiple_of(c * CHUNK, CHUNK), CHUNK), :]
        dst = hbuf.at[c, pl.ds(pl.multiple_of(e_z * CHUNK, CHUNK), CHUNK), :]
        pltpu.make_async_copy(src, dst, sem_h.at[c]).start()
        for d in range(1, DP):
            remote(src, dst, snd_i.at[c], sem_h.at[c], sec, (z + d) % DP).start()

    def parts(i, slot):
        rows = pl.ds(pl.multiple_of(z * ROWS, ROWS), ROWS)
        col = lambda n: pl.ds(pl.multiple_of(n * HD, HD), HD)
        out = []
        for p in range(3):
            out.append((qkv_ref.at[0, :, col(10 * p + i)], w.at[slot, rows, pl.ds(HD * p, HD)]))
        out.append((ow_ref.at[0, :, col(i)], w.at[slot, rows, pl.ds(3 * HD, HD)]))
        return out

    def order(n):
        return ((1 - 2 * (n % 2)) * ((n + 1) // 2) + DP) % DP

    def send_round(n):
        d = order(n)
        to_z = (z + d) % DP
        head = parts(to_z, g)

        @pl.when(to_z == z)
        def _():
            for src, dst in head:
                pltpu.make_async_copy(src, dst, sem_z.at[0]).start()

        @pl.when(to_z != z)
        def _():
            for src, dst in head:
                remote(src, dst, sem_w.at[n], sem_z.at[d], sec, to_z).start()

        @pl.when(to_z % GROUP == g)
        def _():
            m = to_z // GROUP
            extra = parts(8 + m, 4)

            @pl.when(to_z == z)
            def _():
                for src, dst in extra[:2]:
                    pltpu.make_async_copy(src, dst, sem_x.at[0]).start()

            @pl.when(to_z != z)
            def _():
                for src, dst in extra[:2]:
                    remote(src, dst, sem_w.at[DP + m], sem_x.at[d], sec, to_z).start()

            for src, dst in extra[2:]:
                remote(src, dst, sem_w.at[DP + 2 + m], sem_x.at[d], y_mate, to_z).start()

    def block(slot, d):
        return w.at[slot, pl.ds(pl.multiple_of((z + DP - d) % DP * ROWS, ROWS), ROWS), :]

    takes = (zg == g) | (zg == slot_y)
    mine = jnp.where(zg == g, 0, 2 * HD)

    def half(d, at):
        rows = pl.ds(pl.multiple_of((z + DP - d) % DP * ROWS, ROWS), ROWS)
        return w.at[4, rows, pl.ds(pl.multiple_of(at, 2 * HD), 2 * HD)]

    for n in range(AHEAD):
        send_round(n)

    @pl.when(feeds)
    def _():
        feed(0)

    def relay(n, _):
        @pl.when(n + AHEAD < DP)
        def _():
            send_round(n + AHEAD)

        @pl.when(n < DP)
        def _():
            d = order(n)
            b = block(g, d)
            drain(b, sem_z.at[d])
            remote(b, b, snd_y.at[d], sem_y.at[d], y_mate, z).start()
            remote(b, b, snd_c.at[d], sem_c.at[d], c_mate, z).start()

            @pl.when(takes)
            def _():
                x = half(d, mine)
                drain(x, sem_x.at[d])
                remote(x, x, snd_yx.at[d], sem_yx.at[d], y_mate, z).start()
                remote(x, x, snd_cx.at[d], sem_cx.at[d], c_mate, z).start()

        @pl.when(n > 0)
        def _():
            d = order(n - 1)
            b = block(slot_y, d)
            drain(b, sem_y.at[d])
            remote(b, b, snd_c2.at[d], sem_c2.at[d], c_mate, z).start()

            @pl.when(takes)
            def _():
                x = half(d, 2 * HD - mine)
                drain(x, sem_yx.at[d])
                remote(x, x, snd_cx2.at[d], sem_cx.at[d], c_mate, z).start()

        return 0

    lax.fori_loop(0, DP + 1, relay, 0)

    drain(span.at[pl.ds(0, 2)], sem_k)
    lane = lax.broadcasted_iota(jnp.int32, (1, HD), 1)
    token = lax.broadcasted_iota(jnp.int32, (LEN, HD), 0).astype(jnp.float32)
    for e in range(2):
        lens = span[e, pl.ds(0, 1), :].astype(jnp.float32)
        key_start = jnp.zeros((LEN, HD), jnp.float32)
        before = jnp.zeros((1, 1), jnp.float32)
        for s in range(1, SPANS):
            start = jnp.sum(jnp.where(lane < s, lens, 0.0), axis=1, keepdims=True)
            key_start = jnp.where(token >= start, before, key_start)
            before = start
        first_ref[e] = key_start

    def arrive(n, _):
        d = order(n)
        drain(block(mate, d), sem_c.at[d])
        drain(block(slot_cy, d), sem_c2.at[d])

        @pl.when(jnp.logical_not(takes))
        def _():
            drain(block(4, d), sem_cx.at[d])

        return 0

    lax.fori_loop(0, DP, arrive, 0)

    row_own = pl.ds(pl.multiple_of(e_own * CHUNK, CHUNK), CHUNK)
    col_own = pl.ds(pl.multiple_of(cc_own * PIECE, PIECE), PIECE)
    scale = HD ** (-0.5)

    def project(c):
        drain(hbuf.at[c], sem_h.at[c])
        values = hbuf[c].astype(jnp.float32)
        mean = jnp.mean(values, axis=-1, keepdims=True)
        centred = values - mean
        var = jnp.mean(centred * centred, axis=-1, keepdims=True)
        normed[...] = (centred * lax.rsqrt(var + 1e-05)).astype(jnp.bfloat16)

        def columns(cols):
            mat = [w[s, :, pl.ds(p * HD, HD * n)] for s, p, n in cols]
            mat = mat[0] if len(mat) == 1 else jnp.concatenate(mat, axis=1)
            return jnp.dot(normed[...], mat, preferred_element_type=jnp.float32).astype(jnp.bfloat16)

        new = pl.ds(pl.multiple_of(c * CHUNK + BACK, CHUNK), CHUNK)
        for s in range(SLOTS):
            qk = columns([(s, 0, 2)])
            qbuf[s] = qk[:, :HD]
            kc[0, new, pl.ds(s * HD, HD)] = qk[:CHUNK, HD:]
            kc[1, new, pl.ds(s * HD, HD)] = qk[CHUNK:, HD:]
        for s in (0, 2, 4):
            n = 2 if s < 4 else 1
            v = columns([(s + i, 2, 1) for i in range(n)])
            vc[0, new, pl.ds(s * HD, n * HD)] = v[:CHUNK]
            vc[1, new, pl.ds(s * HD, n * HD)] = v[CHUNK:]

    def attend(c):
        tok = pl.ds(pl.multiple_of(c * CHUNK, CHUNK), CHUNK)
        first = jnp.concatenate([first_ref[0, tok, :], first_ref[1, tok, :]], axis=0)
        row = lax.broadcasted_iota(jnp.int32, (2 * CHUNK, 2 * KEYS), 0)
        col = lax.broadcasted_iota(jnp.int32, (2 * CHUNK, 2 * KEYS), 1)
        same = (row < CHUNK) == (col < KEYS)
        key_pos = c * CHUNK - BACK + jnp.where(col < KEYS, col, col - KEYS)
        tok_pos = c * CHUNK + jnp.where(row < CHUNK, row, row - CHUNK)
        allowed = same & (key_pos <= tok_pos) & (key_pos.astype(jnp.float32) >= first)

        window = pl.ds(pl.multiple_of(c * CHUNK, CHUNK), KEYS)
        attended = []
        for s in range(SLOTS):
            cols = pl.ds(s * HD, HD)
            keys = jnp.concatenate([kc[0, window, cols], kc[1, window, cols]], axis=0)
            vals = jnp.concatenate([vc[0, window, cols], vc[1, window, cols]], axis=0)
            scores = lax.dot_general(
                qbuf[s], keys, (((1,), (1,)), ((), ())), preferred_element_type=jnp.float32
            ) * scale
            weights = jnp.where(allowed, jnp.exp(scores), 0.0)
            probs = (weights / jnp.sum(weights, axis=-1, keepdims=True)).astype(jnp.bfloat16)
            attended.append(
                jnp.dot(probs, vals, preferred_element_type=jnp.float32).astype(jnp.bfloat16)
            )

        for cc in range(GROUP):
            total = None
            rows = pl.ds(cc * PIECE, PIECE)
            for s in (0, 2, 4):
                n = 2 if s < 4 else 1
                lhs = attended[s] if n == 1 else jnp.concatenate(attended[s : s + n], axis=1)
                rhs = [w[s + i, rows, pl.ds(3 * HD, HD)] for i in range(n)]
                rhs = rhs[0] if n == 1 else jnp.concatenate(rhs, axis=1)
                term = lax.dot_general(
                    lhs, rhs, (((1,), (1,)), ((), ())), preferred_element_type=jnp.float32
                )
                total = term if total is None else total + term
            cols = pl.ds(cc * PIECE, PIECE)
            part[:, cols] = total
            sendb[c, :, cols] = total.astype(jnp.bfloat16)
            for e in range(2):
                to_z = e * GROUP + cc

                @pl.when(z != to_z)
                def _():
                    d = (to_z - z + DP) % DP
                    remote(
                        sendb.at[c, pl.ds(e * CHUNK, CHUNK), cols], rbuf.at[c, d - 1],
                        snd_r.at[c], sem_r.at[c], sec, to_z,
                    ).start()

    def combine(c):
        total = part[row_own, col_own] + hbuf[c, row_own, col_own].astype(jnp.float32)
        drain(rbuf.at[c], sem_r.at[c])
        for d in range(DP - 1):
            total = total + rbuf[c, d].astype(jnp.float32)
        hnew[c] = total.astype(jnp.bfloat16)

        @pl.when(jnp.logical_not(last))
        def _():
            for n in range(DP):
                remote(
                    hnew.at[c], hbuf.at[c, row_own, col_own],
                    snd_h.at[c], sem_h.at[c], base + GROUP + slot_y, (z + n) % DP,
                ).start()

        @pl.when(last)
        def _():
            for k in range(GROUP):
                to_sec = c * GROUP + k
                here = (to_sec == sec) & is_out

                @pl.when(here)
                def _():
                    pltpu.make_async_copy(hnew.at[c], outb.at[:, col_own], sem_o).start()

                @pl.when(jnp.logical_not(here))
                def _():
                    remote(
                        hnew.at[c], outb.at[:, col_own], snd_h.at[c], sem_o, to_sec, out_z
                    ).start()

    def step(c, _):
        @pl.when(feeds & (c < CHUNKS - 1))
        def _():
            feed(c + 1)

        project(c)
        attend(c)
        combine(c)
        return 0

    lax.fori_loop(0, CHUNKS, step, 0)

    drain(outb, sem_o)
    out_ref[...] = outb[...]

    def sent(c, _):
        drain(rbuf.at[c], snd_r.at[c])

        @pl.when(jnp.logical_not(last))
        def _():
            drain(hbuf.at[c], snd_h.at[c])

        @pl.when(last)
        def _():
            own = (c == CHUNKS - 1) & is_out

            @pl.when(own)
            def _():
                drain(outb.at[:, pl.ds(0, 3 * PIECE)], snd_h.at[c])

            @pl.when(jnp.logical_not(own))
            def _():
                drain(outb, snd_h.at[c])

        @pl.when(feeds)
        def _():
            drain(x_ref.at[0, pl.ds(0, LEN - CHUNK), :], snd_i.at[c])

        d = c
        drain(block(g, d), snd_y.at[d])
        drain(block(g, d), snd_c.at[d])
        drain(block(slot_y, d), snd_c2.at[d])

        @pl.when(takes)
        def _():
            drain(half(d, mine), snd_yx.at[d])
            drain(half(d, mine), snd_cx.at[d])
            drain(half(d, mine), snd_cx2.at[d])

        @pl.when(d > 0)
        def _():
            drain(block(g, 0), sem_w.at[d])

        return 0

    lax.fori_loop(0, CHUNKS, sent, 0)
    for m in range(2):
        @pl.when(z != g + GROUP * m)
        def _():
            drain(half(0, 0), sem_w.at[DP + m])

        drain(half(0, 0), sem_w.at[DP + 2 + m])

    @pl.when(own_seq)
    def _():
        for d in range(1, DP):
            drain(span.at[2], snd_k.at[d - 1])


def shards(inputs, span_lengths, qkv_weight, out_weight):
    sections = lax.axis_size("section")
    bf16 = jnp.bfloat16
    dma = lambda *n: pltpu.SemaphoreType.DMA(n)
    out = pl.pallas_call(
        kernel,
        out_shape=jax.ShapeDtypeStruct((CHUNK, WIDTH), bf16),
        in_specs=[
            pl.BlockSpec(memory_space=pl.ANY),
            pl.BlockSpec(memory_space=pltpu.VMEM),
            pl.BlockSpec(memory_space=pl.ANY),
            pl.BlockSpec(memory_space=pl.ANY),
        ],
        out_specs=pl.BlockSpec(memory_space=pltpu.VMEM),
        scratch_shapes=[
            pltpu.VMEM((SLOTS, WIDTH, 4 * HD), bf16),
            pltpu.VMEM((CHUNKS, 2 * CHUNK, WIDTH), bf16),
            pltpu.VMEM((2 * CHUNK, WIDTH), bf16),
            pltpu.VMEM((SLOTS, 2 * CHUNK, HD), bf16),
            pltpu.VMEM((2, LEN + BACK, SLOTS * HD), bf16),
            pltpu.VMEM((2, LEN + BACK, SLOTS * HD), bf16),
            pltpu.VMEM((3, 8, HD), jnp.int32),
            pltpu.VMEM((2, LEN, HD), jnp.float32),
            pltpu.VMEM((2 * CHUNK, WIDTH), jnp.float32),
            pltpu.VMEM((CHUNKS, 2 * CHUNK, WIDTH), bf16),
            pltpu.VMEM((CHUNKS, DP - 1, CHUNK, PIECE), bf16),
            pltpu.VMEM((CHUNKS, CHUNK, PIECE), bf16),
            pltpu.VMEM((CHUNK, WIDTH), bf16),
            dma(DP + 4), dma(DP), dma(DP), dma(DP), dma(DP), dma(DP), dma(DP), dma(DP),
            dma(DP), dma(DP), dma(DP), dma(DP), dma(DP), dma(DP),
            pltpu.SemaphoreType.DMA, dma(DP - 1), dma(CHUNKS), dma(CHUNKS), dma(CHUNKS),
            dma(CHUNKS), dma(CHUNKS), pltpu.SemaphoreType.DMA,
        ],
        compiler_params=pltpu.CompilerParams(
            collective_id=0, has_side_effects=True, vmem_limit_bytes=60 * 1024 * 1024
        ),
    )(inputs, span_lengths, qkv_weight, out_weight)
    rows = LEN // sections
    first = lax.axis_index("section") % (CHUNK // rows) * rows
    return lax.dynamic_slice(out, (first, 0), (rows, WIDTH))[None]


def solution(mesh):
    in_specs = (
        P("dp", None, None),
        P("dp", None),
        P("section", "dp", None),
        P("section", "dp", None),
    )
    out_specs = P("dp", "section", None)
    return jax.shard_map(shards, mesh=mesh, in_specs=in_specs, out_specs=out_specs, check_vma=False)
```

```python
import jax
import jax.numpy as jnp
from jax import lax
from jax.experimental import pallas as pl
from jax.experimental.pallas import tpu as pltpu
from jax.sharding import PartitionSpec as P

HD = 128
GROUP = 4
SPANS = 8
LEN = 128
DP = 8
WIDTH = 2560
ROWS = 320
SLOTS = 5
CHUNK = 16
CHUNKS = LEN // CHUNK
BACK = 48
KEYS = BACK + CHUNK
PIECE = 640
AHEAD = 2
FAR = (0, 3, 1, 2)
MESH = pl.DeviceIdType.MESH


def kernel(
    x_ref, sp_ref, qkv_ref, ow_ref, out_ref,
    w, hbuf, normed, qbuf, kc, vc, span, first_ref, part, sendb, rbuf, hnew, outb,
    sem_w, sem_z, sem_x, sem_y, sem_yx, sem_c, sem_c2, sem_cx,
    snd_y, snd_yx, snd_c, snd_c2, snd_cx, snd_cx2,
    sem_k, snd_k, sem_h, snd_i, sem_r, snd_r, snd_h, sem_o, sem_f, snd_f,
):
    sec = lax.axis_index("section")
    z = lax.axis_index("dp")
    sections = lax.axis_size("section")
    layers = sections // GROUP
    layer = sec // GROUP
    last = layer == layers - 1
    g = sec % GROUP
    base = layer * GROUP
    slot_y = (g + 2) % GROUP
    y_mate = base + slot_y
    mate = g + 1 - 2 * (g % 2)
    c_mate = base + mate
    slot_cy = (mate + 2) % GROUP
    zg = z % GROUP

    q = (g + 2 * (layer % 2)) % GROUP
    q_z = (z % 2) * 2 + z % GROUP // 2
    e_z = z // GROUP
    own_seq = q_z == q
    feeds = (layer >= layers // 2) & (q_z == g)
    e_own = z // GROUP
    cc_own = z % GROUP
    out_z = GROUP * e_own + 2 * (q % 2) + q // 2
    is_out = (out_z == z) & (cc_own == g)

    def remote(src, dst, s_sem, r_sem, to_sec, to_z):
        return pltpu.make_async_remote_copy(
            src_ref=src, dst_ref=dst, send_sem=s_sem, recv_sem=r_sem,
            device_id=(to_sec, to_z), device_id_type=MESH,
        )

    def drain(ref, sem):
        pltpu.make_async_copy(ref, ref, sem).wait()

    barrier = pltpu.get_barrier_semaphore()

    def greet(to_sec, to_z):
        pl.semaphore_signal(barrier, inc=1, device_id=(to_sec, to_z), device_id_type=MESH)

    for d in range(1, DP):
        greet(sec, (z + d) % DP)
    greet(y_mate, z)
    greet(c_mate, z)
    for d in range(1, DP):
        greet(y_mate, (z + d) % DP)

    @pl.when(layer > 0)
    def _():
        for d in range(DP):
            greet(base - GROUP + slot_y, (z + d) % DP)

    @pl.when(layer == 0)
    def _():
        for n in range(layers // 2):
            for e in range(2):
                greet((layers // 2 + n) * GROUP + g, 4 * e + 2 * (g % 2) + g // 2)

    g_out = (q_z + 2 * ((layers - 1) % 2)) % GROUP
    from_sec, from_z = sections - GROUP + g_out, e_z * GROUP + g
    greet(base + GROUP - 1 - g, z)

    @pl.when((from_sec != sec) | (from_z != z))
    def _():
        greet(from_sec, from_z)

    kc[:, pl.ds(0, BACK), :] = jnp.zeros((2, BACK, SLOTS * HD), jnp.bfloat16)
    vc[:, pl.ds(0, BACK), :] = jnp.zeros((2, BACK, SLOTS * HD), jnp.bfloat16)
    span[2] = jnp.zeros((8, HD), jnp.int32)
    span[2, pl.ds(0, 1), pl.ds(0, SPANS)] = sp_ref[...]

    partners = 2 * DP + 1 + jnp.where(last, layers - is_out.astype(jnp.int32), DP)
    pl.semaphore_wait(barrier, partners + DP * feeds.astype(jnp.int32))

    @pl.when(own_seq)
    def _():
        pltpu.make_async_copy(span.at[2], span.at[e_z], sem_k).start()
        for d in range(1, DP):
            remote(span.at[2], span.at[e_z], snd_k.at[d - 1], sem_k, sec, (z + d) % DP).start()

    def feed(c):
        src = x_ref.at[0, pl.ds(pl.multiple_of(c * CHUNK, CHUNK), CHUNK), :]
        dst = hbuf.at[c, pl.ds(pl.multiple_of(e_z * CHUNK, CHUNK), CHUNK), :]
        for d in range(DP):
            remote(src, dst, snd_i.at[c % 2], sem_h.at[c], g, (z + d) % DP).start()

    @pl.when(feeds)
    def _():
        for n in range(2):
            feed(2 * (layer - layers // 2) + n)

    def parts(i, slot):
        rows = pl.ds(pl.multiple_of(z * ROWS, ROWS), ROWS)
        col = lambda n: pl.ds(pl.multiple_of(n * HD, HD), HD)
        out = []
        for p in range(3):
            out.append((qkv_ref.at[0, :, col(10 * p + i)], w.at[slot, rows, pl.ds(HD * p, HD)]))
        out.append((ow_ref.at[0, :, col(i)], w.at[slot, rows, pl.ds(3 * HD, HD)]))
        return out

    def order(n):
        return ((1 - 2 * (n % 2)) * ((n + 1) // 2) + DP) % DP

    def send_round(n):
        d = order(n)
        to_z = (z + d) % DP
        head = parts(to_z, g)

        @pl.when(to_z == z)
        def _():
            for src, dst in head:
                pltpu.make_async_copy(src, dst, sem_z.at[0]).start()

        @pl.when(to_z != z)
        def _():
            for src, dst in head:
                remote(src, dst, sem_w.at[n], sem_z.at[d], sec, to_z).start()

        @pl.when(to_z % GROUP == g)
        def _():
            m = to_z // GROUP
            extra = parts(8 + m, 4)

            @pl.when(to_z == z)
            def _():
                for src, dst in extra[:2]:
                    pltpu.make_async_copy(src, dst, sem_x.at[0]).start()

            @pl.when(to_z != z)
            def _():
                for src, dst in extra[:2]:
                    remote(src, dst, sem_w.at[DP + m], sem_x.at[d], sec, to_z).start()

            for src, dst in extra[2:]:
                remote(src, dst, sem_w.at[DP + 2 + m], sem_x.at[d], y_mate, to_z).start()

    def block(slot, d):
        return w.at[slot, pl.ds(pl.multiple_of((z + DP - d) % DP * ROWS, ROWS), ROWS), :]

    takes = (zg == g) | (zg == slot_y)
    mine = jnp.where(zg == g, 0, 2 * HD)

    def half(d, at):
        rows = pl.ds(pl.multiple_of((z + DP - d) % DP * ROWS, ROWS), ROWS)
        return w.at[4, rows, pl.ds(pl.multiple_of(at, 2 * HD), 2 * HD)]

    for n in range(AHEAD):
        send_round(n)

    def relay(n, _):
        @pl.when(n + AHEAD < DP)
        def _():
            send_round(n + AHEAD)

        @pl.when(n < DP)
        def _():
            d = order(n)
            b = block(g, d)
            drain(b, sem_z.at[d])
            remote(b, b, snd_y.at[d], sem_y.at[d], y_mate, z).start()
            remote(b, b, snd_c.at[d], sem_c.at[d], c_mate, z).start()

            @pl.when(takes)
            def _():
                x = half(d, mine)
                drain(x, sem_x.at[d])
                remote(x, x, snd_yx.at[d], sem_yx.at[d], y_mate, z).start()
                remote(x, x, snd_cx.at[d], sem_cx.at[d], c_mate, z).start()

        @pl.when(n > 0)
        def _():
            d = order(n - 1)
            b = block(slot_y, d)
            drain(b, sem_y.at[d])
            remote(b, b, snd_c2.at[d], sem_c2.at[d], c_mate, z).start()

            @pl.when(takes)
            def _():
                x = half(d, 2 * HD - mine)
                drain(x, sem_yx.at[d])
                remote(x, x, snd_cx2.at[d], sem_cx.at[d], c_mate, z).start()

        return 0

    lax.fori_loop(0, DP + 1, relay, 0)

    drain(span.at[pl.ds(0, 2)], sem_k)
    lane = lax.broadcasted_iota(jnp.int32, (1, HD), 1)
    token = lax.broadcasted_iota(jnp.int32, (LEN, HD), 0).astype(jnp.float32)
    for e in range(2):
        lens = span[e, pl.ds(0, 1), :].astype(jnp.float32)
        key_start = jnp.zeros((LEN, HD), jnp.float32)
        before = jnp.zeros((1, 1), jnp.float32)
        for s in range(1, SPANS):
            start = jnp.sum(jnp.where(lane < s, lens, 0.0), axis=1, keepdims=True)
            key_start = jnp.where(token >= start, before, key_start)
            before = start
        first_ref[e] = key_start

    def arrive(n, _):
        d = order(n)
        drain(block(mate, d), sem_c.at[d])
        drain(block(slot_cy, d), sem_c2.at[d])

        @pl.when(jnp.logical_not(takes))
        def _():
            drain(block(4, d), sem_cx.at[d])

        return 0

    lax.fori_loop(0, DP, arrive, 0)

    row_own = pl.ds(pl.multiple_of(e_own * CHUNK, CHUNK), CHUNK)
    col_own = pl.ds(pl.multiple_of(cc_own * PIECE, PIECE), PIECE)
    scale = HD ** (-0.5)

    def project(c):
        drain(hbuf.at[c], sem_h.at[c])
        values = hbuf[c].astype(jnp.float32)
        mean = jnp.mean(values, axis=-1, keepdims=True)
        centred = values - mean
        var = jnp.mean(centred * centred, axis=-1, keepdims=True)
        normed[...] = (centred * lax.rsqrt(var + 1e-05)).astype(jnp.bfloat16)

        def columns(cols):
            mat = [w[s, :, pl.ds(p * HD, HD * n)] for s, p, n in cols]
            mat = mat[0] if len(mat) == 1 else jnp.concatenate(mat, axis=1)
            return jnp.dot(normed[...], mat, preferred_element_type=jnp.float32).astype(jnp.bfloat16)

        new = pl.ds(pl.multiple_of(c * CHUNK + BACK, CHUNK), CHUNK)
        for s in range(SLOTS):
            qk = columns([(s, 0, 2)])
            qbuf[s] = qk[:, :HD]
            kc[0, new, pl.ds(s * HD, HD)] = qk[:CHUNK, HD:]
            kc[1, new, pl.ds(s * HD, HD)] = qk[CHUNK:, HD:]
        for s in (0, 2, 4):
            n = 2 if s < 4 else 1
            v = columns([(s + i, 2, 1) for i in range(n)])
            vc[0, new, pl.ds(s * HD, n * HD)] = v[:CHUNK]
            vc[1, new, pl.ds(s * HD, n * HD)] = v[CHUNK:]

    def attend(c):
        tok = pl.ds(pl.multiple_of(c * CHUNK, CHUNK), CHUNK)
        first = jnp.concatenate([first_ref[0, tok, :], first_ref[1, tok, :]], axis=0)
        row = lax.broadcasted_iota(jnp.int32, (2 * CHUNK, 2 * KEYS), 0)
        col = lax.broadcasted_iota(jnp.int32, (2 * CHUNK, 2 * KEYS), 1)
        same = (row < CHUNK) == (col < KEYS)
        key_pos = c * CHUNK - BACK + jnp.where(col < KEYS, col, col - KEYS)
        tok_pos = c * CHUNK + jnp.where(row < CHUNK, row, row - CHUNK)
        allowed = same & (key_pos <= tok_pos) & (key_pos.astype(jnp.float32) >= first)

        window = pl.ds(pl.multiple_of(c * CHUNK, CHUNK), KEYS)
        attended = []
        for s in range(SLOTS):
            cols = pl.ds(s * HD, HD)
            keys = jnp.concatenate([kc[0, window, cols], kc[1, window, cols]], axis=0)
            vals = jnp.concatenate([vc[0, window, cols], vc[1, window, cols]], axis=0)
            scores = lax.dot_general(
                qbuf[s], keys, (((1,), (1,)), ((), ())), preferred_element_type=jnp.float32
            ) * scale
            weights = jnp.where(allowed, jnp.exp(scores), 0.0)
            probs = (weights / jnp.sum(weights, axis=-1, keepdims=True)).astype(jnp.bfloat16)
            attended.append(
                jnp.dot(probs, vals, preferred_element_type=jnp.float32).astype(jnp.bfloat16)
            )

        for turn in range(GROUP):
            cc = (cc_own + FAR[turn]) % GROUP
            total = None
            rows = pl.ds(pl.multiple_of(cc * PIECE, PIECE), PIECE)
            for s in (0, 2, 4):
                n = 2 if s < 4 else 1
                lhs = attended[s] if n == 1 else jnp.concatenate(attended[s : s + n], axis=1)
                rhs = [w[s + i, rows, pl.ds(3 * HD, HD)] for i in range(n)]
                rhs = rhs[0] if n == 1 else jnp.concatenate(rhs, axis=1)
                term = lax.dot_general(
                    lhs, rhs, (((1,), (1,)), ((), ())), preferred_element_type=jnp.float32
                )
                total = term if total is None else total + term
            cols = pl.ds(pl.multiple_of(cc * PIECE, PIECE), PIECE)
            part[:, cols] = total
            sendb[c, :, cols] = total.astype(jnp.bfloat16)
            for d in ((FAR[turn] + GROUP), FAR[turn]):
                if d > 0:
                    to_z = (z + d) % DP
                    rows = pl.ds(pl.multiple_of(to_z // GROUP * CHUNK, CHUNK), CHUNK)
                    remote(
                        sendb.at[c, rows, cols], rbuf.at[c, d - 1],
                        snd_r.at[c], sem_r.at[c], sec, to_z,
                    ).start()

    def combine(c):
        total = part[row_own, col_own] + hbuf[c, row_own, col_own].astype(jnp.float32)
        drain(rbuf.at[c], sem_r.at[c])
        for d in range(DP - 1):
            total = total + rbuf[c, d].astype(jnp.float32)
        hnew[c] = total.astype(jnp.bfloat16)

        @pl.when(jnp.logical_not(last))
        def _():
            for n in (4, 3, 5, 2, 6, 1, 7, 0):
                remote(
                    hnew.at[c], hbuf.at[c, row_own, col_own],
                    snd_h.at[c], sem_h.at[c], base + GROUP + slot_y, (z + n) % DP,
                ).start()

        @pl.when(last)
        def _():
            to_sec = c * GROUP + cc_own
            here = (to_sec == sec) & is_out

            @pl.when(here)
            def _():
                pltpu.make_async_copy(hnew.at[c], outb.at[:, col_own], sem_o).start()

            @pl.when(jnp.logical_not(here))
            def _():
                remote(hnew.at[c], outb.at[:, col_own], snd_h.at[c], sem_o, to_sec, out_z).start()

    def step(c, _):
        project(c)
        attend(c)
        combine(c)
        return 0

    lax.fori_loop(0, CHUNKS, step, 0)

    result = outb.at[:, pl.ds(pl.multiple_of(g * PIECE, PIECE), PIECE)]
    drain(result, sem_o)
    for to_sec in (c_mate, y_mate, base + GROUP - 1 - g):
        remote(result, result, snd_f, sem_f, to_sec, z).start()
    drain(outb.at[:, pl.ds(0, 3 * PIECE)], sem_f)
    out_ref[...] = outb[...]
    drain(outb.at[:, pl.ds(0, 3 * PIECE)], snd_f)

    def sent(c, _):
        drain(rbuf.at[c], snd_r.at[c])

        @pl.when(jnp.logical_not(last))
        def _():
            drain(hbuf.at[c], snd_h.at[c])

        @pl.when(last)
        def _():
            @pl.when((c != layer) | jnp.logical_not(is_out))
            def _():
                drain(hnew.at[c], snd_h.at[c])

        d = c
        drain(block(g, d), snd_y.at[d])
        drain(block(g, d), snd_c.at[d])
        drain(block(slot_y, d), snd_c2.at[d])

        @pl.when(takes)
        def _():
            drain(half(d, mine), snd_yx.at[d])
            drain(half(d, mine), snd_cx.at[d])
            drain(half(d, mine), snd_cx2.at[d])

        @pl.when(d > 0)
        def _():
            drain(block(g, 0), sem_w.at[d])

        return 0

    lax.fori_loop(0, CHUNKS, sent, 0)
    for m in range(2):
        @pl.when(z != g + GROUP * m)
        def _():
            drain(half(0, 0), sem_w.at[DP + m])

        drain(half(0, 0), sem_w.at[DP + 2 + m])

    @pl.when(feeds)
    def _():
        for n in range(2):
            drain(x_ref.at[0], snd_i.at[n])

    @pl.when(own_seq)
    def _():
        for d in range(1, DP):
            drain(span.at[2], snd_k.at[d - 1])


def shards(inputs, span_lengths, qkv_weight, out_weight):
    sections = lax.axis_size("section")
    bf16 = jnp.bfloat16
    dma = lambda *n: pltpu.SemaphoreType.DMA(n)
    out = pl.pallas_call(
        kernel,
        out_shape=jax.ShapeDtypeStruct((CHUNK, WIDTH), bf16),
        in_specs=[
            pl.BlockSpec(memory_space=pl.ANY),
            pl.BlockSpec(memory_space=pltpu.VMEM),
            pl.BlockSpec(memory_space=pl.ANY),
            pl.BlockSpec(memory_space=pl.ANY),
        ],
        out_specs=pl.BlockSpec(memory_space=pltpu.VMEM),
        scratch_shapes=[
            pltpu.VMEM((SLOTS, WIDTH, 4 * HD), bf16),
            pltpu.VMEM((CHUNKS, 2 * CHUNK, WIDTH), bf16),
            pltpu.VMEM((2 * CHUNK, WIDTH), bf16),
            pltpu.VMEM((SLOTS, 2 * CHUNK, HD), bf16),
            pltpu.VMEM((2, LEN + BACK, SLOTS * HD), bf16),
            pltpu.VMEM((2, LEN + BACK, SLOTS * HD), bf16),
            pltpu.VMEM((3, 8, HD), jnp.int32),
            pltpu.VMEM((2, LEN, HD), jnp.float32),
            pltpu.VMEM((2 * CHUNK, WIDTH), jnp.float32),
            pltpu.VMEM((CHUNKS, 2 * CHUNK, WIDTH), bf16),
            pltpu.VMEM((CHUNKS, DP - 1, CHUNK, PIECE), bf16),
            pltpu.VMEM((CHUNKS, CHUNK, PIECE), bf16),
            pltpu.VMEM((CHUNK, WIDTH), bf16),
            dma(DP + 4), dma(DP), dma(DP), dma(DP), dma(DP), dma(DP), dma(DP), dma(DP),
            dma(DP), dma(DP), dma(DP), dma(DP), dma(DP), dma(DP),
            pltpu.SemaphoreType.DMA, dma(DP - 1), dma(CHUNKS), dma(CHUNKS), dma(CHUNKS),
            dma(CHUNKS), dma(CHUNKS), pltpu.SemaphoreType.DMA, pltpu.SemaphoreType.DMA,
            pltpu.SemaphoreType.DMA,
        ],
        compiler_params=pltpu.CompilerParams(
            collective_id=0, has_side_effects=True, vmem_limit_bytes=60 * 1024 * 1024
        ),
    )(inputs, span_lengths, qkv_weight, out_weight)
    rows = LEN // sections
    first = lax.axis_index("section") % (CHUNK // rows) * rows
    return lax.dynamic_slice(out, (first, 0), (rows, WIDTH))[None]


def solution(mesh):
    in_specs = (
        P("dp", None, None),
        P("dp", None),
        P("section", "dp", None),
        P("section", "dp", None),
    )
    out_specs = P("dp", "section", None)
    return jax.shard_map(shards, mesh=mesh, in_specs=in_specs, out_specs=out_specs, check_vma=False)
```

```python
import jax
import jax.numpy as jnp
from jax import lax
from jax.experimental import pallas as pl
from jax.experimental.pallas import tpu as pltpu
from jax.sharding import PartitionSpec as P

HD = 128
GROUP = 4
SPANS = 8
LEN = 128
DP = 8
WIDTH = 2560
ROWS = 320
SLOTS = 5
CHUNK = 16
CHUNKS = LEN // CHUNK
BACK = 48
KEYS = BACK + CHUNK
PIECE = 640
AHEAD = 2
FAR = (0, 3, 1, 2)
EARLY = 2
GUEST = 112
MESH = pl.DeviceIdType.MESH


def kernel(
    x_ref, sp_ref, qkv_ref, ow_ref, out_ref,
    w, hbuf, normed, qbuf, kc, vc, span, first_ref, part, sendb, rbuf, hnew, outb,
    staged, sem_s, snd_s, snd_g, sem_gz, sem_gc, snd_gc,
    sem_w, sem_z, sem_x, sem_y, sem_yx, sem_c, sem_c2, sem_cx,
    snd_y, snd_yx, snd_c, snd_c2, snd_cx, snd_cx2,
    sem_k, snd_k, sem_h, snd_i, sem_r, snd_r, snd_h, sem_o, sem_f, snd_f,
):
    sec = lax.axis_index("section")
    z = lax.axis_index("dp")
    sections = lax.axis_size("section")
    layers = sections // GROUP
    layer = sec // GROUP
    last = layer == layers - 1
    g = sec % GROUP
    base = layer * GROUP
    slot_y = (g + 2) % GROUP
    y_mate = base + slot_y
    mate = g + 1 - 2 * (g % 2)
    c_mate = base + mate
    slot_cy = (mate + 2) % GROUP
    zg = z % GROUP

    q = (g + 2 * (layer % 2)) % GROUP
    q_z = (z % 2) * 2 + z % GROUP // 2
    e_z = z // GROUP
    own_seq = q_z == q
    feeds = (layer >= layers // 2) & (q_z == g)
    e_own = z // GROUP
    cc_own = z % GROUP
    out_z = GROUP * e_own + 2 * (q % 2) + q // 2
    is_out = (out_z == z) & (cc_own == g)

    early = layer < EARLY
    helps = layer >= layers - EARLY
    shift = (layers - EARLY) * GROUP

    def remote(src, dst, s_sem, r_sem, to_sec, to_z):
        return pltpu.make_async_remote_copy(
            src_ref=src, dst_ref=dst, send_sem=s_sem, recv_sem=r_sem,
            device_id=(to_sec, to_z), device_id_type=MESH,
        )

    def drain(ref, sem):
        pltpu.make_async_copy(ref, ref, sem).wait()

    barrier = pltpu.get_barrier_semaphore()

    def greet(to_sec, to_z):
        pl.semaphore_signal(barrier, inc=1, device_id=(to_sec, to_z), device_id_type=MESH)

    for d in range(1, DP):
        greet(sec, (z + d) % DP)
    greet(y_mate, z)
    greet(c_mate, z)
    for d in range(1, DP):
        greet(y_mate, (z + d) % DP)

    @pl.when(layer > 0)
    def _():
        for d in range(DP):
            greet(base - GROUP + slot_y, (z + d) % DP)

    @pl.when(early)
    def _():
        for d in range(DP):
            greet(sec + shift, (z + d) % DP)

    @pl.when(helps)
    def _():
        greet(sec - shift, z)
        greet(y_mate - shift, z)

    @pl.when(layer == 0)
    def _():
        for n in range(layers // 2):
            for e in range(2):
                greet((layers // 2 + n) * GROUP + g, 4 * e + 2 * (g % 2) + g // 2)

    g_out = (q_z + 2 * ((layers - 1) % 2)) % GROUP
    from_sec, from_z = sections - GROUP + g_out, e_z * GROUP + g
    greet(base + GROUP - 1 - g, z)

    @pl.when((from_sec != sec) | (from_z != z))
    def _():
        greet(from_sec, from_z)

    kc[:, pl.ds(0, BACK), :] = jnp.zeros((2, BACK, SLOTS * HD), jnp.bfloat16)
    vc[:, pl.ds(0, BACK), :] = jnp.zeros((2, BACK, SLOTS * HD), jnp.bfloat16)
    span[2] = jnp.zeros((8, HD), jnp.int32)
    span[2, pl.ds(0, 1), pl.ds(0, SPANS)] = sp_ref[...]

    partners = 2 * DP + 1 + jnp.where(last, layers - is_out.astype(jnp.int32), DP)
    partners += DP * feeds.astype(jnp.int32) + 2 * early.astype(jnp.int32)
    pl.semaphore_wait(barrier, partners + DP * helps.astype(jnp.int32))

    @pl.when(own_seq)
    def _():
        pltpu.make_async_copy(span.at[2], span.at[e_z], sem_k).start()
        for d in range(1, DP):
            remote(span.at[2], span.at[e_z], snd_k.at[d - 1], sem_k, sec, (z + d) % DP).start()

    def feed(c):
        src = x_ref.at[0, pl.ds(pl.multiple_of(c * CHUNK, CHUNK), CHUNK), :]
        dst = hbuf.at[c, pl.ds(pl.multiple_of(e_z * CHUNK, CHUNK), CHUNK), :]
        for d in range(DP):
            remote(src, dst, snd_i.at[c % 2], sem_h.at[c], g, (z + d) % DP).start()

    @pl.when(feeds)
    def _():
        for n in range(2):
            feed(2 * (layer - layers // 2) + n)

    def hand_over():
        rows = pl.ds(ROWS - GUEST, GUEST)
        for r in range(4):
            cols = pl.ds(10 * HD * r, 10 * HD)
            src = qkv_ref.at[0, rows, cols] if r < 3 else ow_ref.at[0, rows, :]
            for n, to_sec in enumerate((sec, y_mate)):
                remote(
                    src, staged.at[n, r], snd_s.at[n, r], sem_s.at[n, r], to_sec + shift, z
                ).start()

    def pass_on(r, _):
        rows = pl.ds(pl.multiple_of(z * ROWS + ROWS - GUEST, 16), GUEST)
        cols = pl.ds(pl.multiple_of(r * HD, HD), HD)
        for n, slot in enumerate((g, slot_y)):
            drain(staged.at[n, r], sem_s.at[n, r])
            for j in (4, 3, 5, 2, 6, 1, 7, 0):
                to_z = (z + j) % DP
                src = staged.at[n, r, :, pl.ds(pl.multiple_of(to_z * HD, HD), HD)]
                remote(
                    src, w.at[slot, rows, cols], snd_g.at[n, r], sem_gz.at[z], sec - shift, to_z
                ).start()
            for m in range(2):
                src = staged.at[n, r, :, pl.ds((DP + m) * HD, HD)]
                remote(
                    src, w.at[4, rows, cols], snd_g.at[n, r], sem_gz.at[z],
                    sec - shift, slot + GROUP * m,
                ).start()
        return 0

    def take_guests(n, _):
        z_s = (z + DP - order(n)) % DP
        rows = pl.ds(pl.multiple_of(z_s * ROWS + ROWS - GUEST, 16), GUEST)

        @pl.when(takes)
        def _():
            drain(w.at[0, pl.ds(0, 3 * GUEST), :], sem_gz.at[z_s])
            x = w.at[4, rows, :]
            remote(x, x, snd_gc.at[z_s], sem_gc.at[z_s], c_mate, z).start()

        @pl.when(jnp.logical_not(takes))
        def _():
            drain(w.at[0, pl.ds(0, 2 * GUEST), :], sem_gz.at[z_s])

        for slot in (g, slot_y):
            x = w.at[slot, rows, :]
            remote(x, x, snd_gc.at[z_s], sem_gc.at[z_s], c_mate, z).start()
        return 0

    def settle_guests(z_s, _):
        @pl.when(takes)
        def _():
            drain(w.at[0, pl.ds(0, 2 * GUEST), :], sem_gc.at[z_s])
            drain(w.at[0, pl.ds(0, 3 * GUEST), :], snd_gc.at[z_s])

        @pl.when(jnp.logical_not(takes))
        def _():
            drain(w.at[0, pl.ds(0, 3 * GUEST), :], sem_gc.at[z_s])
            drain(w.at[0, pl.ds(0, 2 * GUEST), :], snd_gc.at[z_s])

        return 0

    takes = (zg == g) | (zg == slot_y)
    mine = jnp.where(zg == g, 0, 2 * HD)

    def order(n):
        return ((1 - 2 * (n % 2)) * ((n + 1) // 2) + DP) % DP

    def block(slot, d, size):
        return w.at[slot, pl.ds(pl.multiple_of((z + DP - d) % DP * ROWS, ROWS), size), :]

    def half(d, at, size):
        rows = pl.ds(pl.multiple_of((z + DP - d) % DP * ROWS, ROWS), size)
        return w.at[4, rows, pl.ds(pl.multiple_of(at, 2 * HD), 2 * HD)]

    def relayout(size):
        def parts(i, slot):
            rows = pl.ds(pl.multiple_of(z * ROWS, ROWS), size)
            col = lambda n: pl.ds(pl.multiple_of(n * HD, HD), HD)
            out = []
            for p in range(3):
                out.append((qkv_ref.at[0, pl.ds(0, size), col(10 * p + i)], w.at[slot, rows, pl.ds(HD * p, HD)]))
            out.append((ow_ref.at[0, pl.ds(0, size), col(i)], w.at[slot, rows, pl.ds(3 * HD, HD)]))
            return out

        def send_round(n):
            d = order(n)
            to_z = (z + d) % DP
            head = parts(to_z, g)

            @pl.when(to_z == z)
            def _():
                for src, dst in head:
                    pltpu.make_async_copy(src, dst, sem_z.at[0]).start()

            @pl.when(to_z != z)
            def _():
                for src, dst in head:
                    remote(src, dst, sem_w.at[n], sem_z.at[d], sec, to_z).start()

            @pl.when(to_z % GROUP == g)
            def _():
                m = to_z // GROUP
                extra = parts(8 + m, 4)

                @pl.when(to_z == z)
                def _():
                    for src, dst in extra[:2]:
                        pltpu.make_async_copy(src, dst, sem_x.at[0]).start()

                @pl.when(to_z != z)
                def _():
                    for src, dst in extra[:2]:
                        remote(src, dst, sem_w.at[DP + m], sem_x.at[d], sec, to_z).start()

                for src, dst in extra[2:]:
                    remote(src, dst, sem_w.at[DP + 2 + m], sem_x.at[d], y_mate, to_z).start()

        if size < ROWS:
            hand_over()
        for n in range(AHEAD):
            send_round(n)

        def relay(n, _):
            @pl.when(n + AHEAD < DP)
            def _():
                send_round(n + AHEAD)

            @pl.when(n < DP)
            def _():
                d = order(n)
                b = block(g, d, size)
                drain(b, sem_z.at[d])
                remote(b, b, snd_y.at[d], sem_y.at[d], y_mate, z).start()
                remote(b, b, snd_c.at[d], sem_c.at[d], c_mate, z).start()

                @pl.when(takes)
                def _():
                    x = half(d, mine, size)
                    drain(x, sem_x.at[d])
                    remote(x, x, snd_yx.at[d], sem_yx.at[d], y_mate, z).start()
                    remote(x, x, snd_cx.at[d], sem_cx.at[d], c_mate, z).start()

            @pl.when(n > 0)
            def _():
                d = order(n - 1)
                b = block(slot_y, d, size)
                drain(b, sem_y.at[d])
                remote(b, b, snd_c2.at[d], sem_c2.at[d], c_mate, z).start()

                @pl.when(takes)
                def _():
                    x = half(d, 2 * HD - mine, size)
                    drain(x, sem_yx.at[d])
                    remote(x, x, snd_cx2.at[d], sem_cx.at[d], c_mate, z).start()

            return 0

        lax.fori_loop(0, DP + 1, relay, 0)
        if size < ROWS:
            lax.fori_loop(0, DP, take_guests, 0)

        def arrive(n, _):
            d = order(n)
            drain(block(mate, d, size), sem_c.at[d])
            drain(block(slot_cy, d, size), sem_c2.at[d])

            @pl.when(jnp.logical_not(takes))
            def _():
                drain(block(4, d, size), sem_cx.at[d])

            return 0

        lax.fori_loop(0, DP, arrive, 0)

        if size < ROWS:
            lax.fori_loop(0, DP, settle_guests, 0)

    @pl.when(helps)
    def _():
        lax.fori_loop(0, 4, pass_on, 0)

    @pl.when(early)
    def _():
        relayout(ROWS - GUEST)

    @pl.when(jnp.logical_not(early))
    def _():
        relayout(ROWS)

    drain(span.at[pl.ds(0, 2)], sem_k)
    lane = lax.broadcasted_iota(jnp.int32, (1, HD), 1)
    token = lax.broadcasted_iota(jnp.int32, (LEN, HD), 0).astype(jnp.float32)
    for e in range(2):
        lens = span[e, pl.ds(0, 1), :].astype(jnp.float32)
        key_start = jnp.zeros((LEN, HD), jnp.float32)
        before = jnp.zeros((1, 1), jnp.float32)
        for s in range(1, SPANS):
            start = jnp.sum(jnp.where(lane < s, lens, 0.0), axis=1, keepdims=True)
            key_start = jnp.where(token >= start, before, key_start)
            before = start
        first_ref[e] = key_start

    row_own = pl.ds(pl.multiple_of(e_own * CHUNK, CHUNK), CHUNK)
    col_own = pl.ds(pl.multiple_of(cc_own * PIECE, PIECE), PIECE)
    scale = HD ** (-0.5)

    def project(c):
        drain(hbuf.at[c], sem_h.at[c])
        values = hbuf[c].astype(jnp.float32)
        mean = jnp.mean(values, axis=-1, keepdims=True)
        centred = values - mean
        var = jnp.mean(centred * centred, axis=-1, keepdims=True)
        normed[...] = (centred * lax.rsqrt(var + 1e-05)).astype(jnp.bfloat16)

        def columns(cols):
            mat = [w[s, :, pl.ds(p * HD, HD * n)] for s, p, n in cols]
            mat = mat[0] if len(mat) == 1 else jnp.concatenate(mat, axis=1)
            return jnp.dot(normed[...], mat, preferred_element_type=jnp.float32).astype(jnp.bfloat16)

        new = pl.ds(pl.multiple_of(c * CHUNK + BACK, CHUNK), CHUNK)
        for s in range(SLOTS):
            qk = columns([(s, 0, 2)])
            qbuf[s] = qk[:, :HD]
            kc[0, new, pl.ds(s * HD, HD)] = qk[:CHUNK, HD:]
            kc[1, new, pl.ds(s * HD, HD)] = qk[CHUNK:, HD:]
        for s in (0, 2, 4):
            n = 2 if s < 4 else 1
            v = columns([(s + i, 2, 1) for i in range(n)])
            vc[0, new, pl.ds(s * HD, n * HD)] = v[:CHUNK]
            vc[1, new, pl.ds(s * HD, n * HD)] = v[CHUNK:]

    def attend(c):
        tok = pl.ds(pl.multiple_of(c * CHUNK, CHUNK), CHUNK)
        first = jnp.concatenate([first_ref[0, tok, :], first_ref[1, tok, :]], axis=0)
        row = lax.broadcasted_iota(jnp.int32, (2 * CHUNK, 2 * KEYS), 0)
        col = lax.broadcasted_iota(jnp.int32, (2 * CHUNK, 2 * KEYS), 1)
        same = (row < CHUNK) == (col < KEYS)
        key_pos = c * CHUNK - BACK + jnp.where(col < KEYS, col, col - KEYS)
        tok_pos = c * CHUNK + jnp.where(row < CHUNK, row, row - CHUNK)
        allowed = same & (key_pos <= tok_pos) & (key_pos.astype(jnp.float32) >= first)

        window = pl.ds(pl.multiple_of(c * CHUNK, CHUNK), KEYS)
        attended = []
        for s in range(SLOTS):
            cols = pl.ds(s * HD, HD)
            keys = jnp.concatenate([kc[0, window, cols], kc[1, window, cols]], axis=0)
            vals = jnp.concatenate([vc[0, window, cols], vc[1, window, cols]], axis=0)
            scores = lax.dot_general(
                qbuf[s], keys, (((1,), (1,)), ((), ())), preferred_element_type=jnp.float32
            ) * scale
            weights = jnp.where(allowed, jnp.exp(scores), 0.0)
            probs = (weights / jnp.sum(weights, axis=-1, keepdims=True)).astype(jnp.bfloat16)
            attended.append(
                jnp.dot(probs, vals, preferred_element_type=jnp.float32).astype(jnp.bfloat16)
            )

        for turn in range(GROUP):
            cc = (cc_own + FAR[turn]) % GROUP
            total = None
            rows = pl.ds(pl.multiple_of(cc * PIECE, PIECE), PIECE)
            for s in (0, 2, 4):
                n = 2 if s < 4 else 1
                lhs = attended[s] if n == 1 else jnp.concatenate(attended[s : s + n], axis=1)
                rhs = [w[s + i, rows, pl.ds(3 * HD, HD)] for i in range(n)]
                rhs = rhs[0] if n == 1 else jnp.concatenate(rhs, axis=1)
                term = lax.dot_general(
                    lhs, rhs, (((1,), (1,)), ((), ())), preferred_element_type=jnp.float32
                )
                total = term if total is None else total + term
            cols = pl.ds(pl.multiple_of(cc * PIECE, PIECE), PIECE)
            part[:, cols] = total
            sendb[c, :, cols] = total.astype(jnp.bfloat16)
            for d in ((FAR[turn] + GROUP), FAR[turn]):
                if d > 0:
                    to_z = (z + d) % DP
                    rows = pl.ds(pl.multiple_of(to_z // GROUP * CHUNK, CHUNK), CHUNK)
                    remote(
                        sendb.at[c, rows, cols], rbuf.at[c, d - 1],
                        snd_r.at[c], sem_r.at[c], sec, to_z,
                    ).start()

    def combine(c):
        total = part[row_own, col_own] + hbuf[c, row_own, col_own].astype(jnp.float32)
        drain(rbuf.at[c], sem_r.at[c])
        for d in range(DP - 1):
            total = total + rbuf[c, d].astype(jnp.float32)
        hnew[c] = total.astype(jnp.bfloat16)

        @pl.when(jnp.logical_not(last))
        def _():
            for n in (4, 3, 5, 2, 6, 1, 7, 0):
                remote(
                    hnew.at[c], hbuf.at[c, row_own, col_own],
                    snd_h.at[c], sem_h.at[c], base + GROUP + slot_y, (z + n) % DP,
                ).start()

        @pl.when(last)
        def _():
            to_sec = c * GROUP + cc_own
            here = (to_sec == sec) & is_out

            @pl.when(here)
            def _():
                pltpu.make_async_copy(hnew.at[c], outb.at[:, col_own], sem_o).start()

            @pl.when(jnp.logical_not(here))
            def _():
                remote(hnew.at[c], outb.at[:, col_own], snd_h.at[c], sem_o, to_sec, out_z).start()

    def step(c, _):
        project(c)
        attend(c)
        combine(c)
        return 0

    lax.fori_loop(0, CHUNKS, step, 0)

    result = outb.at[:, pl.ds(pl.multiple_of(g * PIECE, PIECE), PIECE)]
    drain(result, sem_o)
    for to_sec in (c_mate, y_mate, base + GROUP - 1 - g):
        remote(result, result, snd_f, sem_f, to_sec, z).start()
    drain(outb.at[:, pl.ds(0, 3 * PIECE)], sem_f)
    out_ref[...] = outb[...]
    drain(outb.at[:, pl.ds(0, 3 * PIECE)], snd_f)

    def sent(c, _):
        drain(rbuf.at[c], snd_r.at[c])

        @pl.when(jnp.logical_not(last))
        def _():
            drain(hbuf.at[c], snd_h.at[c])

        @pl.when(last)
        def _():
            @pl.when((c != layer) | jnp.logical_not(is_out))
            def _():
                drain(hnew.at[c], snd_h.at[c])

        return 0

    lax.fori_loop(0, CHUNKS, sent, 0)

    def sent_weights(size):
        def one(d, _):
            drain(block(g, d, size), snd_y.at[d])
            drain(block(g, d, size), snd_c.at[d])
            drain(block(slot_y, d, size), snd_c2.at[d])

            @pl.when(takes)
            def _():
                drain(half(d, mine, size), snd_yx.at[d])
                drain(half(d, mine, size), snd_cx.at[d])
                drain(half(d, mine, size), snd_cx2.at[d])

            @pl.when(d > 0)
            def _():
                drain(block(g, 0, size), sem_w.at[d])

            return 0

        lax.fori_loop(0, DP, one, 0)
        for m in range(2):
            @pl.when(z != g + GROUP * m)
            def _():
                drain(half(0, 0, size), sem_w.at[DP + m])

            drain(half(0, 0, size), sem_w.at[DP + 2 + m])

        if size < ROWS:
            for n in range(2):
                for r in range(4):
                    drain(staged.at[n, r], snd_s.at[n, r])

    @pl.when(early)
    def _():
        sent_weights(ROWS - GUEST)

    @pl.when(jnp.logical_not(early))
    def _():
        sent_weights(ROWS)

    @pl.when(helps)
    def _():
        for n in range(2):
            for r in range(4):
                drain(staged.at[n, r], snd_g.at[n, r])

    @pl.when(feeds)
    def _():
        for n in range(2):
            drain(x_ref.at[0], snd_i.at[n])

    @pl.when(own_seq)
    def _():
        for d in range(1, DP):
            drain(span.at[2], snd_k.at[d - 1])


def shards(inputs, span_lengths, qkv_weight, out_weight):
    sections = lax.axis_size("section")
    bf16 = jnp.bfloat16
    dma = lambda *n: pltpu.SemaphoreType.DMA(n)
    out = pl.pallas_call(
        kernel,
        out_shape=jax.ShapeDtypeStruct((CHUNK, WIDTH), bf16),
        in_specs=[
            pl.BlockSpec(memory_space=pl.ANY),
            pl.BlockSpec(memory_space=pltpu.VMEM),
            pl.BlockSpec(memory_space=pl.ANY),
            pl.BlockSpec(memory_space=pl.ANY),
        ],
        out_specs=pl.BlockSpec(memory_space=pltpu.VMEM),
        scratch_shapes=[
            pltpu.VMEM((SLOTS, WIDTH, 4 * HD), bf16),
            pltpu.VMEM((CHUNKS, 2 * CHUNK, WIDTH), bf16),
            pltpu.VMEM((2 * CHUNK, WIDTH), bf16),
            pltpu.VMEM((SLOTS, 2 * CHUNK, HD), bf16),
            pltpu.VMEM((2, LEN + BACK, SLOTS * HD), bf16),
            pltpu.VMEM((2, LEN + BACK, SLOTS * HD), bf16),
            pltpu.VMEM((3, 8, HD), jnp.int32),
            pltpu.VMEM((2, LEN, HD), jnp.float32),
            pltpu.VMEM((2 * CHUNK, WIDTH), jnp.float32),
            pltpu.VMEM((CHUNKS, 2 * CHUNK, WIDTH), bf16),
            pltpu.VMEM((CHUNKS, DP - 1, CHUNK, PIECE), bf16),
            pltpu.VMEM((CHUNKS, CHUNK, PIECE), bf16),
            pltpu.VMEM((CHUNK, WIDTH), bf16),
            pltpu.VMEM((2, 4, GUEST, 10 * HD), bf16),
            dma(2, 4), dma(2, 4), dma(2, 4), dma(DP), dma(DP), dma(DP),
            dma(DP + 4), dma(DP), dma(DP), dma(DP), dma(DP), dma(DP), dma(DP), dma(DP),
            dma(DP), dma(DP), dma(DP), dma(DP), dma(DP), dma(DP),
            pltpu.SemaphoreType.DMA, dma(DP - 1), dma(CHUNKS), dma(CHUNKS), dma(CHUNKS),
            dma(CHUNKS), dma(CHUNKS), pltpu.SemaphoreType.DMA, pltpu.SemaphoreType.DMA,
            pltpu.SemaphoreType.DMA,
        ],
        compiler_params=pltpu.CompilerParams(
            collective_id=0, has_side_effects=True, vmem_limit_bytes=60 * 1024 * 1024
        ),
    )(inputs, span_lengths, qkv_weight, out_weight)
    rows = LEN // sections
    first = lax.axis_index("section") % (CHUNK // rows) * rows
    return lax.dynamic_slice(out, (first, 0), (rows, WIDTH))[None]


def solution(mesh):
    in_specs = (
        P("dp", None, None),
        P("dp", None),
        P("section", "dp", None),
        P("section", "dp", None),
    )
    out_specs = P("dp", "section", None)
    return jax.shard_map(shards, mesh=mesh, in_specs=in_specs, out_specs=out_specs, check_vma=False)
```

```python
import jax
import jax.numpy as jnp
from jax import lax
from jax.experimental import pallas as pl
from jax.experimental.pallas import tpu as pltpu
from jax.sharding import PartitionSpec as P

HD = 128
GROUP = 4
SPANS = 8
LEN = 128
DP = 8
WIDTH = 2560
ROWS = 320
SLOTS = 5
CHUNK = 16
CHUNKS = LEN // CHUNK
BACK = 48
KEYS = BACK + CHUNK
PIECE = 640
AHEAD = 2
FAR = (0, 3, 1, 2)
EARLY = 2
GUEST = 16
MESH = pl.DeviceIdType.MESH


def kernel(
    x_ref, sp_ref, qkv_ref, ow_ref, out_ref,
    w, hbuf, normed, qbuf, kc, vc, span, first_ref, part, sendb, rbuf, hnew, outb,
    staged, extras, sem_s, snd_s, snd_g, sem_gz, sem_gc, snd_gc,
    sem_w, sem_z, sem_x, sem_y, sem_yx, sem_c, sem_c2, sem_cx,
    snd_y, snd_yx, snd_c, snd_c2, snd_cx, snd_cx2,
    sem_k, snd_k, sem_h, snd_i, sem_r, snd_r, snd_h, sem_o, sem_f, snd_f,
):
    sec = lax.axis_index("section")
    z = lax.axis_index("dp")
    sections = lax.axis_size("section")
    layers = sections // GROUP
    layer = sec // GROUP
    last = layer == layers - 1
    g = sec % GROUP
    base = layer * GROUP
    slot_y = (g + 2) % GROUP
    y_mate = base + slot_y
    mate = g + 1 - 2 * (g % 2)
    c_mate = base + mate
    slot_cy = (mate + 2) % GROUP
    zg = z % GROUP

    q = (g + 2 * (layer % 2)) % GROUP
    q_z = (z % 2) * 2 + z % GROUP // 2
    e_z = z // GROUP
    own_seq = q_z == q
    feeds = (layer >= layers // 2) & (q_z == g)
    e_own = z // GROUP
    cc_own = z % GROUP
    out_z = GROUP * e_own + 2 * (q % 2) + q // 2
    is_out = (out_z == z) & (cc_own == g)

    early = layer < EARLY
    helps = layer >= layers - EARLY
    shift = (layers - EARLY) * GROUP

    def remote(src, dst, s_sem, r_sem, to_sec, to_z):
        return pltpu.make_async_remote_copy(
            src_ref=src, dst_ref=dst, send_sem=s_sem, recv_sem=r_sem,
            device_id=(to_sec, to_z), device_id_type=MESH,
        )

    def drain(ref, sem):
        pltpu.make_async_copy(ref, ref, sem).wait()

    barrier = pltpu.get_barrier_semaphore()

    def greet(to_sec, to_z):
        pl.semaphore_signal(barrier, inc=1, device_id=(to_sec, to_z), device_id_type=MESH)

    for d in range(1, DP):
        greet(sec, (z + d) % DP)
    greet(y_mate, z)
    greet(c_mate, z)
    for d in range(1, DP):
        greet(y_mate, (z + d) % DP)

    @pl.when(layer > 0)
    def _():
        for d in range(DP):
            greet(base - GROUP + slot_y, (z + d) % DP)

    @pl.when(early)
    def _():
        for d in range(DP):
            greet(sec + shift, (z + d) % DP)

    @pl.when(helps)
    def _():
        greet(sec - shift, z)
        greet(y_mate - shift, z)

    @pl.when(layer == 0)
    def _():
        for n in range(layers // 2):
            for e in range(2):
                greet((layers // 2 + n) * GROUP + g, 4 * e + 2 * (g % 2) + g // 2)

    g_out = (q_z + 2 * ((layers - 1) % 2)) % GROUP
    from_sec, from_z = sections - GROUP + g_out, e_z * GROUP + g
    greet(base + GROUP - 1 - g, z)

    @pl.when((from_sec != sec) | (from_z != z))
    def _():
        greet(from_sec, from_z)

    kc[:, pl.ds(0, BACK), :] = jnp.zeros((2, BACK, SLOTS * HD), jnp.bfloat16)
    vc[:, pl.ds(0, BACK), :] = jnp.zeros((2, BACK, SLOTS * HD), jnp.bfloat16)
    span[2] = jnp.zeros((8, HD), jnp.int32)
    span[2, pl.ds(0, 1), pl.ds(0, SPANS)] = sp_ref[...]

    partners = 2 * DP + 1 + jnp.where(last, layers - is_out.astype(jnp.int32), DP)
    partners += DP * feeds.astype(jnp.int32) + 2 * early.astype(jnp.int32)
    pl.semaphore_wait(barrier, partners + DP * helps.astype(jnp.int32))

    @pl.when(own_seq)
    def _():
        pltpu.make_async_copy(span.at[2], span.at[e_z], sem_k).start()
        for d in range(1, DP):
            remote(span.at[2], span.at[e_z], snd_k.at[d - 1], sem_k, sec, (z + d) % DP).start()

    def feed(c):
        src = x_ref.at[0, pl.ds(pl.multiple_of(c * CHUNK, CHUNK), CHUNK), :]
        dst = hbuf.at[c, pl.ds(pl.multiple_of(e_z * CHUNK, CHUNK), CHUNK), :]
        for d in range(DP):
            remote(src, dst, snd_i.at[c % 2], sem_h.at[c], g, (z + d) % DP).start()

    @pl.when(feeds)
    def _():
        for n in range(2):
            feed(2 * (layer - layers // 2) + n)

    def hand_over():
        for r in range(4):
            for kind in range(2):
                rows = pl.ds(ROWS - GUEST, GUEST) if kind == 0 else pl.ds(0, ROWS)
                first, count = (0, DP * HD) if kind == 0 else (DP * HD, 2 * HD)
                if r < 3:
                    src = qkv_ref.at[0, rows, pl.ds(10 * HD * r + first, count)]
                else:
                    src = ow_ref.at[0, rows, pl.ds(first, count)]
                for n, to_sec in enumerate((sec, y_mate)):
                    dst = (staged if kind == 0 else extras).at[n, r]
                    remote(
                        src, dst, snd_s.at[kind, n, r], sem_s.at[kind, n, r], to_sec + shift, z
                    ).start()

    def pass_on(r, _):
        some = pl.ds(pl.multiple_of(z * ROWS + ROWS - GUEST, 16), GUEST)
        every = pl.ds(pl.multiple_of(z * ROWS, 16), ROWS)
        cols = pl.ds(pl.multiple_of(r * HD, HD), HD)
        for n, slot in enumerate((g, slot_y)):
            drain(staged.at[n, r], sem_s.at[0, n, r])
            for j in (4, 3, 5, 2, 6, 1, 7, 0):
                to_z = (z + j) % DP
                src = staged.at[n, r, :, pl.ds(pl.multiple_of(to_z * HD, HD), HD)]
                remote(
                    src, w.at[slot, some, cols], snd_g.at[0, n, r], sem_gz.at[z],
                    sec - shift, to_z,
                ).start()
        for n, slot in enumerate((g, slot_y)):
            drain(extras.at[n, r], sem_s.at[1, n, r])
            for m in range(2):
                src = extras.at[n, r, :, pl.ds(m * HD, HD)]
                remote(
                    src, w.at[4, every, cols], snd_g.at[1, n, r], sem_gz.at[z],
                    sec - shift, slot + GROUP * m,
                ).start()
        return 0

    def take_guests(n, _):
        z_s = (z + DP - order(n)) % DP
        rows = pl.ds(pl.multiple_of(z_s * ROWS + ROWS - GUEST, 16), GUEST)

        @pl.when(takes)
        def _():
            drain(w.at[0, pl.ds(0, 2 * GUEST + ROWS), :], sem_gz.at[z_s])
            x = block(4, order(n), ROWS)
            remote(x, x, snd_gc.at[z_s], sem_gc.at[z_s], c_mate, z).start()

        @pl.when(jnp.logical_not(takes))
        def _():
            drain(w.at[0, pl.ds(0, 2 * GUEST), :], sem_gz.at[z_s])

        for slot in (g, slot_y):
            x = w.at[slot, rows, :]
            remote(x, x, snd_gc.at[z_s], sem_gc.at[z_s], c_mate, z).start()
        return 0

    def settle_guests(z_s, _):
        @pl.when(takes)
        def _():
            drain(w.at[0, pl.ds(0, 2 * GUEST), :], sem_gc.at[z_s])
            drain(w.at[0, pl.ds(0, 2 * GUEST + ROWS), :], snd_gc.at[z_s])

        @pl.when(jnp.logical_not(takes))
        def _():
            drain(w.at[0, pl.ds(0, 2 * GUEST + ROWS), :], sem_gc.at[z_s])
            drain(w.at[0, pl.ds(0, 2 * GUEST), :], snd_gc.at[z_s])

        return 0

    takes = (zg == g) | (zg == slot_y)
    mine = jnp.where(zg == g, 0, 2 * HD)

    def order(n):
        return ((1 - 2 * (n % 2)) * ((n + 1) // 2) + DP) % DP

    def block(slot, d, size):
        return w.at[slot, pl.ds(pl.multiple_of((z + DP - d) % DP * ROWS, ROWS), size), :]

    def half(d, at, size):
        rows = pl.ds(pl.multiple_of((z + DP - d) % DP * ROWS, ROWS), size)
        return w.at[4, rows, pl.ds(pl.multiple_of(at, 2 * HD), 2 * HD)]

    def relayout(size):
        def parts(i, slot):
            rows = pl.ds(pl.multiple_of(z * ROWS, ROWS), size)
            col = lambda n: pl.ds(pl.multiple_of(n * HD, HD), HD)
            out = []
            for p in range(3):
                out.append((qkv_ref.at[0, pl.ds(0, size), col(10 * p + i)], w.at[slot, rows, pl.ds(HD * p, HD)]))
            out.append((ow_ref.at[0, pl.ds(0, size), col(i)], w.at[slot, rows, pl.ds(3 * HD, HD)]))
            return out

        def send_round(n):
            d = order(n)
            to_z = (z + d) % DP
            head = parts(to_z, g)

            @pl.when(to_z == z)
            def _():
                for src, dst in head:
                    pltpu.make_async_copy(src, dst, sem_z.at[0]).start()

            @pl.when(to_z != z)
            def _():
                for src, dst in head:
                    remote(src, dst, sem_w.at[n], sem_z.at[d], sec, to_z).start()

            @pl.when((to_z % GROUP == g) & (size == ROWS))
            def _():
                m = to_z // GROUP
                extra = parts(8 + m, 4)

                @pl.when(to_z == z)
                def _():
                    for src, dst in extra[:2]:
                        pltpu.make_async_copy(src, dst, sem_x.at[0]).start()

                @pl.when(to_z != z)
                def _():
                    for src, dst in extra[:2]:
                        remote(src, dst, sem_w.at[DP + m], sem_x.at[d], sec, to_z).start()

                for src, dst in extra[2:]:
                    remote(src, dst, sem_w.at[DP + 2 + m], sem_x.at[d], y_mate, to_z).start()

        if size < ROWS:
            hand_over()
        for n in range(AHEAD):
            send_round(n)

        def relay(n, _):
            @pl.when(n + AHEAD < DP)
            def _():
                send_round(n + AHEAD)

            @pl.when(n < DP)
            def _():
                d = order(n)
                b = block(g, d, size)
                drain(b, sem_z.at[d])
                remote(b, b, snd_y.at[d], sem_y.at[d], y_mate, z).start()
                remote(b, b, snd_c.at[d], sem_c.at[d], c_mate, z).start()

                @pl.when(takes & (size == ROWS))
                def _():
                    x = half(d, mine, size)
                    drain(x, sem_x.at[d])
                    remote(x, x, snd_yx.at[d], sem_yx.at[d], y_mate, z).start()
                    remote(x, x, snd_cx.at[d], sem_cx.at[d], c_mate, z).start()

            @pl.when(n > 0)
            def _():
                d = order(n - 1)
                b = block(slot_y, d, size)
                drain(b, sem_y.at[d])
                remote(b, b, snd_c2.at[d], sem_c2.at[d], c_mate, z).start()

                @pl.when(takes & (size == ROWS))
                def _():
                    x = half(d, 2 * HD - mine, size)
                    drain(x, sem_yx.at[d])
                    remote(x, x, snd_cx2.at[d], sem_cx.at[d], c_mate, z).start()

            return 0

        lax.fori_loop(0, DP + 1, relay, 0)
        if size < ROWS:
            lax.fori_loop(0, DP, take_guests, 0)

        def arrive(n, _):
            d = order(n)
            drain(block(mate, d, size), sem_c.at[d])
            drain(block(slot_cy, d, size), sem_c2.at[d])

            @pl.when(jnp.logical_not(takes) & (size == ROWS))
            def _():
                drain(block(4, d, size), sem_cx.at[d])

            return 0

        lax.fori_loop(0, DP, arrive, 0)

        if size < ROWS:
            lax.fori_loop(0, DP, settle_guests, 0)

    @pl.when(helps)
    def _():
        lax.fori_loop(0, 4, pass_on, 0)

    @pl.when(early)
    def _():
        relayout(ROWS - GUEST)

    @pl.when(jnp.logical_not(early))
    def _():
        relayout(ROWS)

    drain(span.at[pl.ds(0, 2)], sem_k)
    lane = lax.broadcasted_iota(jnp.int32, (1, HD), 1)
    token = lax.broadcasted_iota(jnp.int32, (LEN, HD), 0).astype(jnp.float32)
    for e in range(2):
        lens = span[e, pl.ds(0, 1), :].astype(jnp.float32)
        key_start = jnp.zeros((LEN, HD), jnp.float32)
        before = jnp.zeros((1, 1), jnp.float32)
        for s in range(1, SPANS):
            start = jnp.sum(jnp.where(lane < s, lens, 0.0), axis=1, keepdims=True)
            key_start = jnp.where(token >= start, before, key_start)
            before = start
        first_ref[e] = key_start

    row_own = pl.ds(pl.multiple_of(e_own * CHUNK, CHUNK), CHUNK)
    col_own = pl.ds(pl.multiple_of(cc_own * PIECE, PIECE), PIECE)
    scale = HD ** (-0.5)

    def project(c):
        drain(hbuf.at[c], sem_h.at[c])
        values = hbuf[c].astype(jnp.float32)
        mean = jnp.mean(values, axis=-1, keepdims=True)
        centred = values - mean
        var = jnp.mean(centred * centred, axis=-1, keepdims=True)
        normed[...] = (centred * lax.rsqrt(var + 1e-05)).astype(jnp.bfloat16)

        def columns(cols):
            mat = [w[s, :, pl.ds(p * HD, HD * n)] for s, p, n in cols]
            mat = mat[0] if len(mat) == 1 else jnp.concatenate(mat, axis=1)
            return jnp.dot(normed[...], mat, preferred_element_type=jnp.float32).astype(jnp.bfloat16)

        new = pl.ds(pl.multiple_of(c * CHUNK + BACK, CHUNK), CHUNK)
        for s in range(SLOTS):
            qk = columns([(s, 0, 2)])
            qbuf[s] = qk[:, :HD]
            kc[0, new, pl.ds(s * HD, HD)] = qk[:CHUNK, HD:]
            kc[1, new, pl.ds(s * HD, HD)] = qk[CHUNK:, HD:]
        for s in (0, 2, 4):
            n = 2 if s < 4 else 1
            v = columns([(s + i, 2, 1) for i in range(n)])
            vc[0, new, pl.ds(s * HD, n * HD)] = v[:CHUNK]
            vc[1, new, pl.ds(s * HD, n * HD)] = v[CHUNK:]

    def attend(c):
        tok = pl.ds(pl.multiple_of(c * CHUNK, CHUNK), CHUNK)
        first = jnp.concatenate([first_ref[0, tok, :], first_ref[1, tok, :]], axis=0)
        row = lax.broadcasted_iota(jnp.int32, (2 * CHUNK, 2 * KEYS), 0)
        col = lax.broadcasted_iota(jnp.int32, (2 * CHUNK, 2 * KEYS), 1)
        same = (row < CHUNK) == (col < KEYS)
        key_pos = c * CHUNK - BACK + jnp.where(col < KEYS, col, col - KEYS)
        tok_pos = c * CHUNK + jnp.where(row < CHUNK, row, row - CHUNK)
        allowed = same & (key_pos <= tok_pos) & (key_pos.astype(jnp.float32) >= first)

        window = pl.ds(pl.multiple_of(c * CHUNK, CHUNK), KEYS)
        scores, vals = [], []
        for s in range(SLOTS):
            cols = pl.ds(s * HD, HD)
            keys = jnp.concatenate([kc[0, window, cols], kc[1, window, cols]], axis=0)
            vals.append(jnp.concatenate([vc[0, window, cols], vc[1, window, cols]], axis=0))
            scores.append(lax.dot_general(
                qbuf[s], keys, (((1,), (1,)), ((), ())), preferred_element_type=jnp.float32
            ))
        weights = [jnp.where(allowed, jnp.exp(x * scale), 0.0) for x in scores]
        sums = [jnp.sum(x, axis=-1, keepdims=True) for x in weights]
        probs = [(x / y).astype(jnp.bfloat16) for x, y in zip(weights, sums)]
        attended = [
            jnp.dot(x, y, preferred_element_type=jnp.float32).astype(jnp.bfloat16)
            for x, y in zip(probs, vals)
        ]

        for turn in range(GROUP):
            cc = (cc_own + FAR[turn]) % GROUP
            total = None
            rows = pl.ds(pl.multiple_of(cc * PIECE, PIECE), PIECE)
            for s in (0, 2, 4):
                n = 2 if s < 4 else 1
                lhs = attended[s] if n == 1 else jnp.concatenate(attended[s : s + n], axis=1)
                rhs = [w[s + i, rows, pl.ds(3 * HD, HD)] for i in range(n)]
                rhs = rhs[0] if n == 1 else jnp.concatenate(rhs, axis=1)
                term = lax.dot_general(
                    lhs, rhs, (((1,), (1,)), ((), ())), preferred_element_type=jnp.float32
                )
                total = term if total is None else total + term
            cols = pl.ds(pl.multiple_of(cc * PIECE, PIECE), PIECE)
            part[:, cols] = total
            sendb[c, :, cols] = total.astype(jnp.bfloat16)
            for d in ((FAR[turn] + GROUP), FAR[turn]):
                if d > 0:
                    to_z = (z + d) % DP
                    rows = pl.ds(pl.multiple_of(to_z // GROUP * CHUNK, CHUNK), CHUNK)
                    remote(
                        sendb.at[c, rows, cols], rbuf.at[c, d - 1],
                        snd_r.at[c], sem_r.at[c], sec, to_z,
                    ).start()

    def combine(c):
        total = part[row_own, col_own] + hbuf[c, row_own, col_own].astype(jnp.float32)
        drain(rbuf.at[c], sem_r.at[c])
        for d in range(DP - 1):
            total = total + rbuf[c, d].astype(jnp.float32)
        hnew[c] = total.astype(jnp.bfloat16)

        @pl.when(jnp.logical_not(last))
        def _():
            for n in (4, 3, 5, 2, 6, 1, 7, 0):
                remote(
                    hnew.at[c], hbuf.at[c, row_own, col_own],
                    snd_h.at[c], sem_h.at[c], base + GROUP + slot_y, (z + n) % DP,
                ).start()

        @pl.when(last)
        def _():
            to_sec = c * GROUP + cc_own
            here = (to_sec == sec) & is_out

            @pl.when(here)
            def _():
                pltpu.make_async_copy(hnew.at[c], outb.at[:, col_own], sem_o).start()

            @pl.when(jnp.logical_not(here))
            def _():
                remote(hnew.at[c], outb.at[:, col_own], snd_h.at[c], sem_o, to_sec, out_z).start()

    def step(c, _):
        project(c)
        attend(c)
        combine(c)
        return 0

    lax.fori_loop(0, CHUNKS, step, 0)

    result = outb.at[:, pl.ds(pl.multiple_of(g * PIECE, PIECE), PIECE)]
    drain(result, sem_o)
    for to_sec in (c_mate, y_mate, base + GROUP - 1 - g):
        remote(result, result, snd_f, sem_f, to_sec, z).start()
    drain(outb.at[:, pl.ds(0, 3 * PIECE)], sem_f)
    out_ref[...] = outb[...]
    drain(outb.at[:, pl.ds(0, 3 * PIECE)], snd_f)

    def sent(c, _):
        drain(rbuf.at[c], snd_r.at[c])

        @pl.when(jnp.logical_not(last))
        def _():
            drain(hbuf.at[c], snd_h.at[c])

        @pl.when(last)
        def _():
            @pl.when((c != layer) | jnp.logical_not(is_out))
            def _():
                drain(hnew.at[c], snd_h.at[c])

        return 0

    lax.fori_loop(0, CHUNKS, sent, 0)

    def sent_weights(size):
        def one(d, _):
            drain(block(g, d, size), snd_y.at[d])
            drain(block(g, d, size), snd_c.at[d])
            drain(block(slot_y, d, size), snd_c2.at[d])

            @pl.when(takes & (size == ROWS))
            def _():
                drain(half(d, mine, size), snd_yx.at[d])
                drain(half(d, mine, size), snd_cx.at[d])
                drain(half(d, mine, size), snd_cx2.at[d])

            @pl.when(d > 0)
            def _():
                drain(block(g, 0, size), sem_w.at[d])

            return 0

        lax.fori_loop(0, DP, one, 0)
        if size == ROWS:
            for m in range(2):
                @pl.when(z != g + GROUP * m)
                def _():
                    drain(half(0, 0, size), sem_w.at[DP + m])

                drain(half(0, 0, size), sem_w.at[DP + 2 + m])
        else:
            for n in range(2):
                for r in range(4):
                    drain(staged.at[n, r], snd_s.at[0, n, r])
                    drain(extras.at[n, r], snd_s.at[1, n, r])

    @pl.when(early)
    def _():
        sent_weights(ROWS - GUEST)

    @pl.when(jnp.logical_not(early))
    def _():
        sent_weights(ROWS)

    @pl.when(helps)
    def _():
        for n in range(2):
            for r in range(4):
                drain(staged.at[n, r], snd_g.at[0, n, r])
                drain(extras.at[n, r], snd_g.at[1, n, r])

    @pl.when(feeds)
    def _():
        for n in range(2):
            drain(x_ref.at[0], snd_i.at[n])

    @pl.when(own_seq)
    def _():
        for d in range(1, DP):
            drain(span.at[2], snd_k.at[d - 1])


def shards(inputs, span_lengths, qkv_weight, out_weight):
    sections = lax.axis_size("section")
    bf16 = jnp.bfloat16
    dma = lambda *n: pltpu.SemaphoreType.DMA(n)
    out = pl.pallas_call(
        kernel,
        out_shape=jax.ShapeDtypeStruct((CHUNK, WIDTH), bf16),
        in_specs=[
            pl.BlockSpec(memory_space=pl.ANY),
            pl.BlockSpec(memory_space=pltpu.VMEM),
            pl.BlockSpec(memory_space=pl.ANY),
            pl.BlockSpec(memory_space=pl.ANY),
        ],
        out_specs=pl.BlockSpec(memory_space=pltpu.VMEM),
        scratch_shapes=[
            pltpu.VMEM((SLOTS, WIDTH, 4 * HD), bf16),
            pltpu.VMEM((CHUNKS, 2 * CHUNK, WIDTH), bf16),
            pltpu.VMEM((2 * CHUNK, WIDTH), bf16),
            pltpu.VMEM((SLOTS, 2 * CHUNK, HD), bf16),
            pltpu.VMEM((2, LEN + BACK, SLOTS * HD), bf16),
            pltpu.VMEM((2, LEN + BACK, SLOTS * HD), bf16),
            pltpu.VMEM((3, 8, HD), jnp.int32),
            pltpu.VMEM((2, LEN, HD), jnp.float32),
            pltpu.VMEM((2 * CHUNK, WIDTH), jnp.float32),
            pltpu.VMEM((CHUNKS, 2 * CHUNK, WIDTH), bf16),
            pltpu.VMEM((CHUNKS, DP - 1, CHUNK, PIECE), bf16),
            pltpu.VMEM((CHUNKS, CHUNK, PIECE), bf16),
            pltpu.VMEM((CHUNK, WIDTH), bf16),
            pltpu.VMEM((2, 4, GUEST, DP * HD), bf16),
            pltpu.VMEM((2, 4, ROWS, 2 * HD), bf16),
            dma(2, 2, 4), dma(2, 2, 4), dma(2, 2, 4), dma(DP), dma(DP), dma(DP),
            dma(DP + 4), dma(DP), dma(DP), dma(DP), dma(DP), dma(DP), dma(DP), dma(DP),
            dma(DP), dma(DP), dma(DP), dma(DP), dma(DP), dma(DP),
            pltpu.SemaphoreType.DMA, dma(DP - 1), dma(CHUNKS), dma(CHUNKS), dma(CHUNKS),
            dma(CHUNKS), dma(CHUNKS), pltpu.SemaphoreType.DMA, pltpu.SemaphoreType.DMA,
            pltpu.SemaphoreType.DMA,
        ],
        compiler_params=pltpu.CompilerParams(
            collective_id=0, has_side_effects=True, vmem_limit_bytes=60 * 1024 * 1024
        ),
    )(inputs, span_lengths, qkv_weight, out_weight)
    rows = LEN // sections
    first = lax.axis_index("section") % (CHUNK // rows) * rows
    return lax.dynamic_slice(out, (first, 0), (rows, WIDTH))[None]


def solution(mesh):
    in_specs = (
        P("dp", None, None),
        P("dp", None),
        P("section", "dp", None),
        P("section", "dp", None),
    )
    out_specs = P("dp", "section", None)
    return jax.shard_map(shards, mesh=mesh, in_specs=in_specs, out_specs=out_specs, check_vma=False)
```

```python
import jax
import jax.numpy as jnp
from jax import lax
from jax.experimental import pallas as pl
from jax.experimental.pallas import tpu as pltpu
from jax.sharding import PartitionSpec as P

HD = 128
GROUP = 4
SPANS = 8
LEN = 128
DP = 8
WIDTH = 2560
ROWS = 320
SLOTS = 5
CHUNK = 16
CHUNKS = LEN // CHUNK
BACK = 48
KEYS = BACK + CHUNK
PIECE = 640
AHEAD = 2
FAR = (0, 3, 1, 2)
EARLY = 2
GUEST = 16
MESH = pl.DeviceIdType.MESH


def kernel(
    x_ref, sp_ref, qkv_ref, ow_ref, out_ref,
    w, hbuf, normed, qbuf, kc, vc, span, first_ref, part, sendb, rbuf, hnew, outb,
    staged, extras, sem_s, snd_s, snd_g, sem_gz, sem_gc, snd_gc,
    sem_w, sem_z, sem_x, sem_y, sem_yx, sem_c, sem_c2, sem_cx,
    snd_y, snd_yx, snd_c, snd_c2, snd_cx, snd_cx2,
    sem_k, snd_k, sem_h, snd_i, sem_r, snd_r, snd_h, sem_o, sem_f, snd_f,
):
    sec = lax.axis_index("section")
    z = lax.axis_index("dp")
    sections = lax.axis_size("section")
    layers = sections // GROUP
    layer = sec // GROUP
    last = layer == layers - 1
    g = sec % GROUP
    base = layer * GROUP
    slot_y = (g + 2) % GROUP
    y_mate = base + slot_y
    mate = g + 1 - 2 * (g % 2)
    c_mate = base + mate
    slot_cy = (mate + 2) % GROUP
    zg = z % GROUP

    q = (g + 2 * (layer % 2)) % GROUP
    q_z = (z % 2) * 2 + z % GROUP // 2
    e_z = z // GROUP
    own_seq = q_z == q
    feeds = (layer >= layers // 2) & (q_z == g)
    e_own = z // GROUP
    cc_own = z % GROUP
    out_z = GROUP * e_own + 2 * (q % 2) + q // 2
    is_out = out_z == z
    next_sec = base + GROUP + slot_y
    peers = [(z + d) % DP for d in range(DP)]
    peer_rows = [pl.ds(pl.multiple_of(p // GROUP * CHUNK, CHUNK), CHUNK) for p in peers]

    early = layer < EARLY
    helps = layer >= layers - EARLY
    shift = (layers - EARLY) * GROUP

    def remote(src, dst, s_sem, r_sem, to_sec, to_z):
        return pltpu.make_async_remote_copy(
            src_ref=src, dst_ref=dst, send_sem=s_sem, recv_sem=r_sem,
            device_id=(to_sec, to_z), device_id_type=MESH,
        )

    def drain(ref, sem):
        pltpu.make_async_copy(ref, ref, sem).wait()

    barrier = pltpu.get_barrier_semaphore()

    def greet(to_sec, to_z):
        pl.semaphore_signal(barrier, inc=1, device_id=(to_sec, to_z), device_id_type=MESH)

    for d in range(1, DP):
        greet(sec, (z + d) % DP)
    greet(y_mate, z)
    greet(c_mate, z)
    for d in range(1, DP):
        greet(y_mate, (z + d) % DP)

    @pl.when(layer > 0)
    def _():
        for d in range(DP):
            greet(base - GROUP + slot_y, (z + d) % DP)

    @pl.when(early)
    def _():
        for d in range(DP):
            greet(sec + shift, (z + d) % DP)

    @pl.when(helps)
    def _():
        greet(sec - shift, z)
        greet(y_mate - shift, z)

    @pl.when(layer == 0)
    def _():
        for n in range(layers // 2):
            for e in range(2):
                greet((layers // 2 + n) * GROUP + g, 4 * e + 2 * (g % 2) + g // 2)

    g_out = (q_z + 2 * ((layers - 1) % 2)) % GROUP
    from_sec = sections - GROUP + g_out

    @pl.when(jnp.logical_not(last))
    def _():
        greet(base + GROUP - 1 - g, z)
        greet(from_sec, e_z * GROUP + g)

    @pl.when(last)
    def _():
        for cc in range(GROUP):
            from_z = e_z * GROUP + cc

            @pl.when((from_sec != sec) | (from_z != z))
            def _():
                greet(from_sec, from_z)

    kc[:, pl.ds(0, BACK), :] = jnp.zeros((2, BACK, SLOTS * HD), jnp.bfloat16)
    vc[:, pl.ds(0, BACK), :] = jnp.zeros((2, BACK, SLOTS * HD), jnp.bfloat16)
    span[2] = jnp.zeros((8, HD), jnp.int32)
    span[2, pl.ds(0, 1), pl.ds(0, SPANS)] = sp_ref[...]

    partners = 2 * DP + jnp.where(last, layers - 1 + GROUP - is_out.astype(jnp.int32), DP + 1)
    partners += DP * feeds.astype(jnp.int32) + 2 * early.astype(jnp.int32)
    pl.semaphore_wait(barrier, partners + DP * helps.astype(jnp.int32))

    @pl.when(own_seq)
    def _():
        pltpu.make_async_copy(span.at[2], span.at[e_z], sem_k).start()
        for d in range(1, DP):
            remote(span.at[2], span.at[e_z], snd_k.at[d - 1], sem_k, sec, (z + d) % DP).start()

    def feed(c):
        src = x_ref.at[0, pl.ds(pl.multiple_of(c * CHUNK, CHUNK), CHUNK), :]
        dst = hbuf.at[c, pl.ds(pl.multiple_of(e_z * CHUNK, CHUNK), CHUNK), :]
        for d in range(DP):
            remote(src, dst, snd_i.at[c % 2], sem_h.at[c], g, (z + d) % DP).start()

    @pl.when(feeds)
    def _():
        for n in range(2):
            feed(2 * (layer - layers // 2) + n)

    def hand_over():
        for r in range(4):
            for kind in range(2):
                rows = pl.ds(ROWS - GUEST, GUEST) if kind == 0 else pl.ds(0, ROWS)
                first, count = (0, DP * HD) if kind == 0 else (DP * HD, 2 * HD)
                if r < 3:
                    src = qkv_ref.at[0, rows, pl.ds(10 * HD * r + first, count)]
                else:
                    src = ow_ref.at[0, rows, pl.ds(first, count)]
                for n, to_sec in enumerate((sec, y_mate)):
                    dst = (staged if kind == 0 else extras).at[n, r]
                    remote(
                        src, dst, snd_s.at[kind, n, r], sem_s.at[kind, n, r], to_sec + shift, z
                    ).start()

    def pass_on(r, _):
        some = pl.ds(pl.multiple_of(z * ROWS + ROWS - GUEST, 16), GUEST)
        every = pl.ds(pl.multiple_of(z * ROWS, 16), ROWS)
        cols = pl.ds(pl.multiple_of(r * HD, HD), HD)
        for n, slot in enumerate((g, slot_y)):
            drain(staged.at[n, r], sem_s.at[0, n, r])
            for j in (4, 3, 5, 2, 6, 1, 7, 0):
                to_z = (z + j) % DP
                src = staged.at[n, r, :, pl.ds(pl.multiple_of(to_z * HD, HD), HD)]
                remote(
                    src, w.at[slot, some, cols], snd_g.at[0, n, r], sem_gz.at[z],
                    sec - shift, to_z,
                ).start()
        for n, slot in enumerate((g, slot_y)):
            drain(extras.at[n, r], sem_s.at[1, n, r])
            for m in range(2):
                src = extras.at[n, r, :, pl.ds(m * HD, HD)]
                remote(
                    src, w.at[4, every, cols], snd_g.at[1, n, r], sem_gz.at[z],
                    sec - shift, slot + GROUP * m,
                ).start()
        return 0

    def take_guests(n, _):
        z_s = (z + DP - order(n)) % DP
        rows = pl.ds(pl.multiple_of(z_s * ROWS + ROWS - GUEST, 16), GUEST)

        @pl.when(takes)
        def _():
            drain(w.at[0, pl.ds(0, 2 * GUEST + ROWS), :], sem_gz.at[z_s])
            x = block(4, order(n), ROWS)
            remote(x, x, snd_gc.at[z_s], sem_gc.at[z_s], c_mate, z).start()

        @pl.when(jnp.logical_not(takes))
        def _():
            drain(w.at[0, pl.ds(0, 2 * GUEST), :], sem_gz.at[z_s])

        for slot in (g, slot_y):
            x = w.at[slot, rows, :]
            remote(x, x, snd_gc.at[z_s], sem_gc.at[z_s], c_mate, z).start()
        return 0

    def settle_guests(z_s, _):
        @pl.when(takes)
        def _():
            drain(w.at[0, pl.ds(0, 2 * GUEST), :], sem_gc.at[z_s])
            drain(w.at[0, pl.ds(0, 2 * GUEST + ROWS), :], snd_gc.at[z_s])

        @pl.when(jnp.logical_not(takes))
        def _():
            drain(w.at[0, pl.ds(0, 2 * GUEST + ROWS), :], sem_gc.at[z_s])
            drain(w.at[0, pl.ds(0, 2 * GUEST), :], snd_gc.at[z_s])

        return 0

    takes = (zg == g) | (zg == slot_y)
    mine = jnp.where(zg == g, 0, 2 * HD)

    def order(n):
        return ((1 - 2 * (n % 2)) * ((n + 1) // 2) + DP) % DP

    def block(slot, d, size):
        return w.at[slot, pl.ds(pl.multiple_of((z + DP - d) % DP * ROWS, ROWS), size), :]

    def half(d, at, size):
        rows = pl.ds(pl.multiple_of((z + DP - d) % DP * ROWS, ROWS), size)
        return w.at[4, rows, pl.ds(pl.multiple_of(at, 2 * HD), 2 * HD)]

    def relayout(size):
        def parts(i, slot):
            rows = pl.ds(pl.multiple_of(z * ROWS, ROWS), size)
            col = lambda n: pl.ds(pl.multiple_of(n * HD, HD), HD)
            out = []
            for p in range(3):
                out.append((qkv_ref.at[0, pl.ds(0, size), col(10 * p + i)], w.at[slot, rows, pl.ds(HD * p, HD)]))
            out.append((ow_ref.at[0, pl.ds(0, size), col(i)], w.at[slot, rows, pl.ds(3 * HD, HD)]))
            return out

        def send_round(n):
            d = order(n)
            to_z = (z + d) % DP
            head = parts(to_z, g)

            @pl.when(to_z == z)
            def _():
                for src, dst in head:
                    pltpu.make_async_copy(src, dst, sem_z.at[0]).start()

            @pl.when(to_z != z)
            def _():
                for src, dst in head:
                    remote(src, dst, sem_w.at[n], sem_z.at[d], sec, to_z).start()

            @pl.when((to_z % GROUP == g) & (size == ROWS))
            def _():
                m = to_z // GROUP
                extra = parts(8 + m, 4)

                @pl.when(to_z == z)
                def _():
                    for src, dst in extra[:2]:
                        pltpu.make_async_copy(src, dst, sem_x.at[0]).start()

                @pl.when(to_z != z)
                def _():
                    for src, dst in extra[:2]:
                        remote(src, dst, sem_w.at[DP + m], sem_x.at[d], sec, to_z).start()

                for src, dst in extra[2:]:
                    remote(src, dst, sem_w.at[DP + 2 + m], sem_x.at[d], y_mate, to_z).start()

        for n in range(AHEAD):
            send_round(n)
        if size < ROWS:
            hand_over()

        def relay(n, _):
            @pl.when(n + AHEAD < DP)
            def _():
                send_round(n + AHEAD)

            @pl.when(n < DP)
            def _():
                d = order(n)
                b = block(g, d, size)
                drain(b, sem_z.at[d])
                remote(b, b, snd_y.at[d], sem_y.at[d], y_mate, z).start()
                remote(b, b, snd_c.at[d], sem_c.at[d], c_mate, z).start()

                @pl.when(takes & (size == ROWS))
                def _():
                    x = half(d, mine, size)
                    drain(x, sem_x.at[d])
                    remote(x, x, snd_yx.at[d], sem_yx.at[d], y_mate, z).start()
                    remote(x, x, snd_cx.at[d], sem_cx.at[d], c_mate, z).start()

            @pl.when(n > 0)
            def _():
                d = order(n - 1)
                b = block(slot_y, d, size)
                drain(b, sem_y.at[d])
                remote(b, b, snd_c2.at[d], sem_c2.at[d], c_mate, z).start()

                @pl.when(takes & (size == ROWS))
                def _():
                    x = half(d, 2 * HD - mine, size)
                    drain(x, sem_yx.at[d])
                    remote(x, x, snd_cx2.at[d], sem_cx.at[d], c_mate, z).start()

            return 0

        lax.fori_loop(0, DP + 1, relay, 0)
        if size < ROWS:
            lax.fori_loop(0, DP, take_guests, 0)

        def arrive(n, _):
            d = order(n)
            drain(block(mate, d, size), sem_c.at[d])
            drain(block(slot_cy, d, size), sem_c2.at[d])

            @pl.when(jnp.logical_not(takes) & (size == ROWS))
            def _():
                drain(block(4, d, size), sem_cx.at[d])

            return 0

        lax.fori_loop(0, DP, arrive, 0)

        if size < ROWS:
            lax.fori_loop(0, DP, settle_guests, 0)

    @pl.when(helps)
    def _():
        lax.fori_loop(0, 4, pass_on, 0)

    @pl.when(early)
    def _():
        relayout(ROWS - GUEST)

    @pl.when(jnp.logical_not(early))
    def _():
        relayout(ROWS)

    drain(span.at[pl.ds(0, 2)], sem_k)
    lane = lax.broadcasted_iota(jnp.int32, (1, HD), 1)
    token = lax.broadcasted_iota(jnp.int32, (LEN, HD), 0).astype(jnp.float32)
    for e in range(2):
        lens = span[e, pl.ds(0, 1), :].astype(jnp.float32)
        key_start = jnp.zeros((LEN, HD), jnp.float32)
        before = jnp.zeros((1, 1), jnp.float32)
        for s in range(1, SPANS):
            start = jnp.sum(jnp.where(lane < s, lens, 0.0), axis=1, keepdims=True)
            key_start = jnp.where(token >= start, before, key_start)
            before = start
        first_ref[e] = key_start

    row_own = pl.ds(pl.multiple_of(e_own * CHUNK, CHUNK), CHUNK)
    col_own = pl.ds(pl.multiple_of(cc_own * PIECE, PIECE), PIECE)
    scale = HD ** (-0.5)

    def project(c):
        drain(hbuf.at[c], sem_h.at[c])
        values = hbuf[c].astype(jnp.float32)
        mean = jnp.mean(values, axis=-1, keepdims=True)
        centred = values - mean
        var = jnp.mean(centred * centred, axis=-1, keepdims=True)
        normed[...] = (centred * lax.rsqrt(var + 1e-05)).astype(jnp.bfloat16)

        def columns(cols):
            mat = [w[s, :, pl.ds(p * HD, HD * n)] for s, p, n in cols]
            mat = mat[0] if len(mat) == 1 else jnp.concatenate(mat, axis=1)
            return jnp.dot(normed[...], mat, preferred_element_type=jnp.float32).astype(jnp.bfloat16)

        new = pl.ds(pl.multiple_of(c * CHUNK + BACK, CHUNK), CHUNK)
        for s in range(SLOTS):
            qk = columns([(s, 0, 2)])
            qbuf[s] = qk[:, :HD]
            kc[0, new, pl.ds(s * HD, HD)] = qk[:CHUNK, HD:]
            kc[1, new, pl.ds(s * HD, HD)] = qk[CHUNK:, HD:]
        for s in (0, 2, 4):
            n = 2 if s < 4 else 1
            v = columns([(s + i, 2, 1) for i in range(n)])
            vc[0, new, pl.ds(s * HD, n * HD)] = v[:CHUNK]
            vc[1, new, pl.ds(s * HD, n * HD)] = v[CHUNK:]

    def attend(c):
        tok = pl.ds(pl.multiple_of(c * CHUNK, CHUNK), CHUNK)
        first = jnp.concatenate([first_ref[0, tok, :], first_ref[1, tok, :]], axis=0)
        row = lax.broadcasted_iota(jnp.int32, (2 * CHUNK, 2 * KEYS), 0)
        col = lax.broadcasted_iota(jnp.int32, (2 * CHUNK, 2 * KEYS), 1)
        same = (row < CHUNK) == (col < KEYS)
        key_pos = c * CHUNK - BACK + jnp.where(col < KEYS, col, col - KEYS)
        tok_pos = c * CHUNK + jnp.where(row < CHUNK, row, row - CHUNK)
        allowed = same & (key_pos <= tok_pos) & (key_pos.astype(jnp.float32) >= first)

        window = pl.ds(pl.multiple_of(c * CHUNK, CHUNK), KEYS)
        scores, vals = [], []
        for s in range(SLOTS):
            cols = pl.ds(s * HD, HD)
            keys = jnp.concatenate([kc[0, window, cols], kc[1, window, cols]], axis=0)
            vals.append(jnp.concatenate([vc[0, window, cols], vc[1, window, cols]], axis=0))
            scores.append(lax.dot_general(
                qbuf[s], keys, (((1,), (1,)), ((), ())), preferred_element_type=jnp.float32
            ))
        weights = [jnp.where(allowed, jnp.exp(x * scale), 0.0) for x in scores]
        sums = [jnp.sum(x, axis=-1, keepdims=True) for x in weights]
        probs = [(x / y).astype(jnp.bfloat16) for x, y in zip(weights, sums)]
        attended = [
            jnp.dot(x, y, preferred_element_type=jnp.float32).astype(jnp.bfloat16)
            for x, y in zip(probs, vals)
        ]

        for turn in range(GROUP):
            cc = (cc_own + FAR[turn]) % GROUP
            total = None
            rows = pl.ds(pl.multiple_of(cc * PIECE, PIECE), PIECE)
            for s in (0, 2, 4):
                n = 2 if s < 4 else 1
                lhs = attended[s] if n == 1 else jnp.concatenate(attended[s : s + n], axis=1)
                rhs = [w[s + i, rows, pl.ds(3 * HD, HD)] for i in range(n)]
                rhs = rhs[0] if n == 1 else jnp.concatenate(rhs, axis=1)
                term = lax.dot_general(
                    lhs, rhs, (((1,), (1,)), ((), ())), preferred_element_type=jnp.float32
                )
                total = term if total is None else total + term
            cols = pl.ds(pl.multiple_of(cc * PIECE, PIECE), PIECE)
            if turn == 0:
                part[...] = total
            sendb[c, :, cols] = total.astype(jnp.bfloat16)
            for d in ((FAR[turn] + GROUP), FAR[turn]):
                if d > 0:
                    remote(
                        sendb.at[c, peer_rows[d], cols], rbuf.at[c, d - 1],
                        snd_r.at[c], sem_r.at[c], sec, peers[d],
                    ).start()

    def combine(c):
        total = part[row_own, :] + hbuf[c, row_own, col_own].astype(jnp.float32)
        drain(rbuf.at[c], sem_r.at[c])
        for d in range(DP - 1):
            total = total + rbuf[c, d].astype(jnp.float32)
        hnew[c] = total.astype(jnp.bfloat16)

        @pl.when(jnp.logical_not(last))
        def _():
            for n in (4, 3, 5, 2, 6, 1, 7, 0):
                remote(
                    hnew.at[c], hbuf.at[c, row_own, col_own],
                    snd_h.at[c], sem_h.at[c], next_sec, peers[n],
                ).start()

        @pl.when(last & (c < CHUNKS - 1))
        def _():
            to_sec = c * GROUP + cc_own
            remote(hnew.at[c], outb.at[:, col_own], snd_h.at[c], sem_o, to_sec, out_z).start()

        @pl.when(last & (c == CHUNKS - 1))
        def _():
            for n in range(GROUP):
                here = (n == g) & is_out

                @pl.when(here)
                def _():
                    pltpu.make_async_copy(hnew.at[c], outb.at[:, col_own], sem_o).start()

                @pl.when(jnp.logical_not(here))
                def _():
                    to_sec = sections - GROUP + n
                    remote(
                        hnew.at[c], outb.at[:, col_own], snd_h.at[c], sem_o, to_sec, out_z
                    ).start()

    def step(c, _):
        project(c)
        attend(c)
        combine(c)
        return 0

    lax.fori_loop(0, CHUNKS, step, 0)

    result = outb.at[:, pl.ds(pl.multiple_of(g * PIECE, PIECE), PIECE)]

    @pl.when(jnp.logical_not(last))
    def _():
        drain(result, sem_o)
        for to_sec in (c_mate, y_mate, base + GROUP - 1 - g):
            remote(result, result, snd_f, sem_f, to_sec, z).start()
        drain(outb.at[:, pl.ds(0, 3 * PIECE)], sem_f)
        drain(outb.at[:, pl.ds(0, 3 * PIECE)], snd_f)

    @pl.when(last)
    def _():
        drain(outb, sem_o)

    out_ref[...] = outb[...]

    def sent(c, _):
        drain(rbuf.at[c], snd_r.at[c])

        @pl.when(jnp.logical_not(last))
        def _():
            drain(hbuf.at[c], snd_h.at[c])

        @pl.when(last)
        def _():
            @pl.when(c < CHUNKS - 1)
            def _():
                drain(hnew.at[c], snd_h.at[c])

            @pl.when((c == CHUNKS - 1) & is_out)
            def _():
                drain(outb.at[:, pl.ds(0, 3 * PIECE)], snd_h.at[c])

            @pl.when((c == CHUNKS - 1) & jnp.logical_not(is_out))
            def _():
                drain(outb, snd_h.at[c])

        return 0

    lax.fori_loop(0, CHUNKS, sent, 0)

    def sent_weights(size):
        def one(d, _):
            drain(block(g, d, size), snd_y.at[d])
            drain(block(g, d, size), snd_c.at[d])
            drain(block(slot_y, d, size), snd_c2.at[d])

            @pl.when(takes & (size == ROWS))
            def _():
                drain(half(d, mine, size), snd_yx.at[d])
                drain(half(d, mine, size), snd_cx.at[d])
                drain(half(d, mine, size), snd_cx2.at[d])

            @pl.when(d > 0)
            def _():
                drain(block(g, 0, size), sem_w.at[d])

            return 0

        lax.fori_loop(0, DP, one, 0)
        if size == ROWS:
            for m in range(2):
                @pl.when(z != g + GROUP * m)
                def _():
                    drain(half(0, 0, size), sem_w.at[DP + m])

                drain(half(0, 0, size), sem_w.at[DP + 2 + m])
        else:
            for n in range(2):
                for r in range(4):
                    drain(staged.at[n, r], snd_s.at[0, n, r])
                    drain(extras.at[n, r], snd_s.at[1, n, r])

    @pl.when(early)
    def _():
        sent_weights(ROWS - GUEST)

    @pl.when(jnp.logical_not(early))
    def _():
        sent_weights(ROWS)

    @pl.when(helps)
    def _():
        for n in range(2):
            for r in range(4):
                drain(staged.at[n, r], snd_g.at[0, n, r])
                drain(extras.at[n, r], snd_g.at[1, n, r])

    @pl.when(feeds)
    def _():
        for n in range(2):
            drain(x_ref.at[0], snd_i.at[n])

    @pl.when(own_seq)
    def _():
        for d in range(1, DP):
            drain(span.at[2], snd_k.at[d - 1])


def shards(inputs, span_lengths, qkv_weight, out_weight):
    sections = lax.axis_size("section")
    bf16 = jnp.bfloat16
    dma = lambda *n: pltpu.SemaphoreType.DMA(n)
    out = pl.pallas_call(
        kernel,
        out_shape=jax.ShapeDtypeStruct((CHUNK, WIDTH), bf16),
        in_specs=[
            pl.BlockSpec(memory_space=pl.ANY),
            pl.BlockSpec(memory_space=pltpu.VMEM),
            pl.BlockSpec(memory_space=pl.ANY),
            pl.BlockSpec(memory_space=pl.ANY),
        ],
        out_specs=pl.BlockSpec(memory_space=pltpu.VMEM),
        scratch_shapes=[
            pltpu.VMEM((SLOTS, WIDTH, 4 * HD), bf16),
            pltpu.VMEM((CHUNKS, 2 * CHUNK, WIDTH), bf16),
            pltpu.VMEM((2 * CHUNK, WIDTH), bf16),
            pltpu.VMEM((SLOTS, 2 * CHUNK, HD), bf16),
            pltpu.VMEM((2, LEN + BACK, SLOTS * HD), bf16),
            pltpu.VMEM((2, LEN + BACK, SLOTS * HD), bf16),
            pltpu.VMEM((3, 8, HD), jnp.int32),
            pltpu.VMEM((2, LEN, HD), jnp.float32),
            pltpu.VMEM((2 * CHUNK, PIECE), jnp.float32),
            pltpu.VMEM((CHUNKS, 2 * CHUNK, WIDTH), bf16),
            pltpu.VMEM((CHUNKS, DP - 1, CHUNK, PIECE), bf16),
            pltpu.VMEM((CHUNKS, CHUNK, PIECE), bf16),
            pltpu.VMEM((CHUNK, WIDTH), bf16),
            pltpu.VMEM((2, 4, GUEST, DP * HD), bf16),
            pltpu.VMEM((2, 4, ROWS, 2 * HD), bf16),
            dma(2, 2, 4), dma(2, 2, 4), dma(2, 2, 4), dma(DP), dma(DP), dma(DP),
            dma(DP + 4), dma(DP), dma(DP), dma(DP), dma(DP), dma(DP), dma(DP), dma(DP),
            dma(DP), dma(DP), dma(DP), dma(DP), dma(DP), dma(DP),
            pltpu.SemaphoreType.DMA, dma(DP - 1), dma(CHUNKS), dma(CHUNKS), dma(CHUNKS),
            dma(CHUNKS), dma(CHUNKS), pltpu.SemaphoreType.DMA, pltpu.SemaphoreType.DMA,
            pltpu.SemaphoreType.DMA,
        ],
        compiler_params=pltpu.CompilerParams(
            collective_id=0, has_side_effects=True, vmem_limit_bytes=60 * 1024 * 1024
        ),
    )(inputs, span_lengths, qkv_weight, out_weight)
    rows = LEN // sections
    first = lax.axis_index("section") % (CHUNK // rows) * rows
    return lax.dynamic_slice(out, (first, 0), (rows, WIDTH))[None]


def solution(mesh):
    in_specs = (
        P("dp", None, None),
        P("dp", None),
        P("section", "dp", None),
        P("section", "dp", None),
    )
    out_specs = P("dp", "section", None)
    return jax.shard_map(shards, mesh=mesh, in_specs=in_specs, out_specs=out_specs, check_vma=False)
```

```python
import jax
import jax.numpy as jnp
from jax import lax
from jax.experimental import pallas as pl
from jax.experimental.pallas import tpu as pltpu
from jax.sharding import PartitionSpec as P

HD = 128
GROUP = 4
SPANS = 8
LEN = 128
DP = 8
WIDTH = 2560
ROWS = 320
SLOTS = 5
CHUNK = 16
CHUNKS = LEN // CHUNK
BACK = 48
KEYS = BACK + CHUNK
PIECE = 640
AHEAD = 2
FAR = (0, 3, 1, 2)
EARLY = 2
GUEST = 16
MESH = pl.DeviceIdType.MESH


def kernel(
    x_ref, sp_ref, qkv_ref, ow_ref, out_ref,
    w, hbuf, normed, qbuf, kc, vc, span, first_ref, mask_ref, part, sendb, rbuf, hnew, outb,
    staged, extras, sem_s, snd_s, snd_g, sem_gz, sem_gc, snd_gc,
    sem_w, sem_z, sem_x, sem_y, sem_yx, sem_c, sem_c2, sem_cx,
    snd_y, snd_yx, snd_c, snd_c2, snd_cx, snd_cx2,
    sem_k, snd_k, sem_h, snd_i, sem_r, snd_r, snd_h, sem_o, sem_f, snd_f,
):
    sec = lax.axis_index("section")
    z = lax.axis_index("dp")
    sections = lax.axis_size("section")
    layers = sections // GROUP
    layer = sec // GROUP
    last = layer == layers - 1
    g = sec % GROUP
    base = layer * GROUP
    slot_y = (g + 2) % GROUP
    y_mate = base + slot_y
    mate = g + 1 - 2 * (g % 2)
    c_mate = base + mate
    slot_cy = (mate + 2) % GROUP
    zg = z % GROUP

    q = (g + 2 * (layer % 2)) % GROUP
    q_z = (z % 2) * 2 + z % GROUP // 2
    e_z = z // GROUP
    own_seq = q_z == q
    feeds = (layer >= layers // 2) & (q_z == g)
    e_own = z // GROUP
    cc_own = z % GROUP
    out_z = GROUP * e_own + 2 * (q % 2) + q // 2
    is_out = out_z == z
    next_sec = base + GROUP + slot_y
    peers = [(z + d) % DP for d in range(DP)]
    peer_rows = [pl.ds(pl.multiple_of(p // GROUP * CHUNK, CHUNK), CHUNK) for p in peers]

    early = layer < EARLY
    helps = layer >= layers - EARLY
    shift = (layers - EARLY) * GROUP

    def remote(src, dst, s_sem, r_sem, to_sec, to_z):
        return pltpu.make_async_remote_copy(
            src_ref=src, dst_ref=dst, send_sem=s_sem, recv_sem=r_sem,
            device_id=(to_sec, to_z), device_id_type=MESH,
        )

    def drain(ref, sem):
        pltpu.make_async_copy(ref, ref, sem).wait()

    barrier = pltpu.get_barrier_semaphore()

    def greet(to_sec, to_z):
        pl.semaphore_signal(barrier, inc=1, device_id=(to_sec, to_z), device_id_type=MESH)

    for d in range(1, DP):
        greet(sec, (z + d) % DP)
    greet(y_mate, z)
    greet(c_mate, z)
    for d in range(1, DP):
        greet(y_mate, (z + d) % DP)

    @pl.when(layer > 0)
    def _():
        for d in range(DP):
            greet(base - GROUP + slot_y, (z + d) % DP)

    @pl.when(early)
    def _():
        for d in range(DP):
            greet(sec + shift, (z + d) % DP)

    @pl.when(helps)
    def _():
        greet(sec - shift, z)
        greet(y_mate - shift, z)

    @pl.when(layer == 0)
    def _():
        for n in range(layers // 2):
            for e in range(2):
                greet((layers // 2 + n) * GROUP + g, 4 * e + 2 * (g % 2) + g // 2)

    g_out = (q_z + 2 * ((layers - 1) % 2)) % GROUP
    from_sec = sections - GROUP + g_out

    @pl.when(jnp.logical_not(last))
    def _():
        greet(base + GROUP - 1 - g, z)
        greet(from_sec, e_z * GROUP + g)

    @pl.when(last)
    def _():
        for cc in range(GROUP):
            from_z = e_z * GROUP + cc

            @pl.when((from_sec != sec) | (from_z != z))
            def _():
                greet(from_sec, from_z)

    kc[:, pl.ds(0, BACK), :] = jnp.zeros((2, BACK, SLOTS * HD), jnp.bfloat16)
    vc[:, pl.ds(0, BACK), :] = jnp.zeros((2, BACK, SLOTS * HD), jnp.bfloat16)
    span[2] = jnp.zeros((8, HD), jnp.int32)
    span[2, pl.ds(0, 1), pl.ds(0, SPANS)] = sp_ref[...]

    partners = 2 * DP + jnp.where(last, layers - 1 + GROUP - is_out.astype(jnp.int32), DP + 1)
    partners += DP * feeds.astype(jnp.int32) + 2 * early.astype(jnp.int32)
    pl.semaphore_wait(barrier, partners + DP * helps.astype(jnp.int32))

    @pl.when(own_seq)
    def _():
        pltpu.make_async_copy(span.at[2], span.at[e_z], sem_k).start()
        for d in range(1, DP):
            remote(span.at[2], span.at[e_z], snd_k.at[d - 1], sem_k, sec, (z + d) % DP).start()

    def feed(c):
        src = x_ref.at[0, pl.ds(pl.multiple_of(c * CHUNK, CHUNK), CHUNK), :]
        dst = hbuf.at[c, pl.ds(pl.multiple_of(e_z * CHUNK, CHUNK), CHUNK), :]
        for d in range(DP):
            remote(src, dst, snd_i.at[c % 2], sem_h.at[c], g, (z + d) % DP).start()

    @pl.when(feeds)
    def _():
        for n in range(2):
            feed(2 * (layer - layers // 2) + n)

    def hand_over():
        for r in range(4):
            for kind in range(2):
                rows = pl.ds(ROWS - GUEST, GUEST) if kind == 0 else pl.ds(0, ROWS)
                first, count = (0, DP * HD) if kind == 0 else (DP * HD, 2 * HD)
                if r < 3:
                    src = qkv_ref.at[0, rows, pl.ds(10 * HD * r + first, count)]
                else:
                    src = ow_ref.at[0, rows, pl.ds(first, count)]
                for n, to_sec in enumerate((sec, y_mate)):
                    dst = (staged if kind == 0 else extras).at[n, r]
                    remote(
                        src, dst, snd_s.at[kind, n, r], sem_s.at[kind, n, r], to_sec + shift, z
                    ).start()

    def pass_on(r, _):
        some = pl.ds(pl.multiple_of(z * ROWS + ROWS - GUEST, 16), GUEST)
        every = pl.ds(pl.multiple_of(z * ROWS, 16), ROWS)
        cols = pl.ds(pl.multiple_of(r * HD, HD), HD)
        for n, slot in enumerate((g, slot_y)):
            drain(staged.at[n, r], sem_s.at[0, n, r])
            for j in (4, 3, 5, 2, 6, 1, 7, 0):
                to_z = (z + j) % DP
                src = staged.at[n, r, :, pl.ds(pl.multiple_of(to_z * HD, HD), HD)]
                remote(
                    src, w.at[slot, some, cols], snd_g.at[0, n, r], sem_gz.at[z],
                    sec - shift, to_z,
                ).start()
        for n, slot in enumerate((g, slot_y)):
            drain(extras.at[n, r], sem_s.at[1, n, r])
            for m in range(2):
                src = extras.at[n, r, :, pl.ds(m * HD, HD)]
                remote(
                    src, w.at[4, every, cols], snd_g.at[1, n, r], sem_gz.at[z],
                    sec - shift, slot + GROUP * m,
                ).start()
        return 0

    def take_guests(n, _):
        z_s = (z + DP - order(n)) % DP
        rows = pl.ds(pl.multiple_of(z_s * ROWS + ROWS - GUEST, 16), GUEST)

        @pl.when(takes)
        def _():
            drain(w.at[0, pl.ds(0, 2 * GUEST + ROWS), :], sem_gz.at[z_s])
            x = block(4, order(n), ROWS)
            remote(x, x, snd_gc.at[z_s], sem_gc.at[z_s], c_mate, z).start()

        @pl.when(jnp.logical_not(takes))
        def _():
            drain(w.at[0, pl.ds(0, 2 * GUEST), :], sem_gz.at[z_s])

        for slot in (g, slot_y):
            x = w.at[slot, rows, :]
            remote(x, x, snd_gc.at[z_s], sem_gc.at[z_s], c_mate, z).start()
        return 0

    def settle_guests(z_s, _):
        @pl.when(takes)
        def _():
            drain(w.at[0, pl.ds(0, 2 * GUEST), :], sem_gc.at[z_s])
            drain(w.at[0, pl.ds(0, 2 * GUEST + ROWS), :], snd_gc.at[z_s])

        @pl.when(jnp.logical_not(takes))
        def _():
            drain(w.at[0, pl.ds(0, 2 * GUEST + ROWS), :], sem_gc.at[z_s])
            drain(w.at[0, pl.ds(0, 2 * GUEST), :], snd_gc.at[z_s])

        return 0

    takes = (zg == g) | (zg == slot_y)
    mine = jnp.where(zg == g, 0, 2 * HD)

    def order(n):
        return ((1 - 2 * (n % 2)) * ((n + 1) // 2) + DP) % DP

    def block(slot, d, size):
        return w.at[slot, pl.ds(pl.multiple_of((z + DP - d) % DP * ROWS, ROWS), size), :]

    def half(d, at, size):
        rows = pl.ds(pl.multiple_of((z + DP - d) % DP * ROWS, ROWS), size)
        return w.at[4, rows, pl.ds(pl.multiple_of(at, 2 * HD), 2 * HD)]

    def prepare():
        drain(span.at[pl.ds(0, 2)], sem_k)
        lane = lax.broadcasted_iota(jnp.int32, (1, HD), 1)
        token = lax.broadcasted_iota(jnp.int32, (LEN, HD), 0).astype(jnp.float32)
        for e in range(2):
            lens = span[e, pl.ds(0, 1), :].astype(jnp.float32)
            key_start = jnp.zeros((LEN, HD), jnp.float32)
            before = jnp.zeros((1, 1), jnp.float32)
            for s in range(1, SPANS):
                start = jnp.sum(jnp.where(lane < s, lens, 0.0), axis=1, keepdims=True)
                key_start = jnp.where(token >= start, before, key_start)
                before = start
            first_ref[e] = key_start

        def mask(c, _):
            tok = pl.ds(pl.multiple_of(c * CHUNK, CHUNK), CHUNK)
            first = jnp.concatenate([first_ref[0, tok, :], first_ref[1, tok, :]], axis=0)
            row = lax.broadcasted_iota(jnp.int32, (2 * CHUNK, 2 * KEYS), 0)
            col = lax.broadcasted_iota(jnp.int32, (2 * CHUNK, 2 * KEYS), 1)
            same = (row < CHUNK) == (col < KEYS)
            key_pos = c * CHUNK - BACK + jnp.where(col < KEYS, col, col - KEYS)
            tok_pos = c * CHUNK + jnp.where(row < CHUNK, row, row - CHUNK)
            allowed = same & (key_pos <= tok_pos) & (key_pos.astype(jnp.float32) >= first)
            mask_ref[c] = allowed.astype(jnp.float32)
            return 0

        lax.fori_loop(0, CHUNKS, mask, 0)

    def relayout(size):
        def parts(i, slot):
            rows = pl.ds(pl.multiple_of(z * ROWS, ROWS), size)
            col = lambda n: pl.ds(pl.multiple_of(n * HD, HD), HD)
            out = []
            for p in range(3):
                out.append((qkv_ref.at[0, pl.ds(0, size), col(10 * p + i)], w.at[slot, rows, pl.ds(HD * p, HD)]))
            out.append((ow_ref.at[0, pl.ds(0, size), col(i)], w.at[slot, rows, pl.ds(3 * HD, HD)]))
            return out

        def send_round(n):
            d = order(n)
            to_z = (z + d) % DP
            head = parts(to_z, g)

            @pl.when(to_z == z)
            def _():
                for src, dst in head:
                    pltpu.make_async_copy(src, dst, sem_z.at[0]).start()

            @pl.when(to_z != z)
            def _():
                for src, dst in head:
                    remote(src, dst, sem_w.at[n], sem_z.at[d], sec, to_z).start()

            @pl.when((to_z % GROUP == g) & (size == ROWS))
            def _():
                m = to_z // GROUP
                extra = parts(8 + m, 4)

                @pl.when(to_z == z)
                def _():
                    for src, dst in extra[:2]:
                        pltpu.make_async_copy(src, dst, sem_x.at[0]).start()

                @pl.when(to_z != z)
                def _():
                    for src, dst in extra[:2]:
                        remote(src, dst, sem_w.at[DP + m], sem_x.at[d], sec, to_z).start()

                for src, dst in extra[2:]:
                    remote(src, dst, sem_w.at[DP + 2 + m], sem_x.at[d], y_mate, to_z).start()

        ahead = 3 if size < ROWS else AHEAD
        for n in range(ahead):
            send_round(n)
        if size < ROWS:
            hand_over()

        def relay(n, _):
            @pl.when(n + ahead < DP)
            def _():
                send_round(n + ahead)

            @pl.when(n < DP)
            def _():
                d = order(n)
                b = block(g, d, size)
                drain(b, sem_z.at[d])
                remote(b, b, snd_y.at[d], sem_y.at[d], y_mate, z).start()
                remote(b, b, snd_c.at[d], sem_c.at[d], c_mate, z).start()

                @pl.when(takes & (size == ROWS))
                def _():
                    x = half(d, mine, size)
                    drain(x, sem_x.at[d])
                    remote(x, x, snd_yx.at[d], sem_yx.at[d], y_mate, z).start()
                    remote(x, x, snd_cx.at[d], sem_cx.at[d], c_mate, z).start()

            @pl.when(n > 0)
            def _():
                d = order(n - 1)
                b = block(slot_y, d, size)
                drain(b, sem_y.at[d])
                remote(b, b, snd_c2.at[d], sem_c2.at[d], c_mate, z).start()

                @pl.when(takes & (size == ROWS))
                def _():
                    x = half(d, 2 * HD - mine, size)
                    drain(x, sem_yx.at[d])
                    remote(x, x, snd_cx2.at[d], sem_cx.at[d], c_mate, z).start()

            return 0

        lax.fori_loop(0, DP + 1, relay, 0)
        prepare()
        if size < ROWS:
            lax.fori_loop(0, DP, take_guests, 0)

        def arrive(n, _):
            d = order(n)
            drain(block(mate, d, size), sem_c.at[d])
            drain(block(slot_cy, d, size), sem_c2.at[d])

            @pl.when(jnp.logical_not(takes) & (size == ROWS))
            def _():
                drain(block(4, d, size), sem_cx.at[d])

            return 0

        lax.fori_loop(0, DP, arrive, 0)

        if size < ROWS:
            lax.fori_loop(0, DP, settle_guests, 0)

    @pl.when(helps)
    def _():
        lax.fori_loop(0, 4, pass_on, 0)

    @pl.when(early)
    def _():
        relayout(ROWS - GUEST)

    @pl.when(jnp.logical_not(early))
    def _():
        relayout(ROWS)

    row_own = pl.ds(pl.multiple_of(e_own * CHUNK, CHUNK), CHUNK)
    col_own = pl.ds(pl.multiple_of(cc_own * PIECE, PIECE), PIECE)
    scale = HD ** (-0.5)

    def project(c):
        drain(hbuf.at[c], sem_h.at[c])
        values = hbuf[c].astype(jnp.float32)
        mean = jnp.mean(values, axis=-1, keepdims=True)
        centred = values - mean
        var = jnp.mean(centred * centred, axis=-1, keepdims=True)
        normed[...] = (centred * lax.rsqrt(var + 1e-05)).astype(jnp.bfloat16)

        def columns(cols):
            mat = [w[s, :, pl.ds(p * HD, HD * n)] for s, p, n in cols]
            mat = mat[0] if len(mat) == 1 else jnp.concatenate(mat, axis=1)
            return jnp.dot(normed[...], mat, preferred_element_type=jnp.float32).astype(jnp.bfloat16)

        new = pl.ds(pl.multiple_of(c * CHUNK + BACK, CHUNK), CHUNK)
        for s in range(SLOTS):
            qk = columns([(s, 0, 2)])
            qbuf[s] = qk[:, :HD]
            kc[0, new, pl.ds(s * HD, HD)] = qk[:CHUNK, HD:]
            kc[1, new, pl.ds(s * HD, HD)] = qk[CHUNK:, HD:]
        for s in (0, 2, 4):
            n = 2 if s < 4 else 1
            v = columns([(s + i, 2, 1) for i in range(n)])
            vc[0, new, pl.ds(s * HD, n * HD)] = v[:CHUNK]
            vc[1, new, pl.ds(s * HD, n * HD)] = v[CHUNK:]

    def attend(c):
        allowed = mask_ref[c] > 0.0
        window = pl.ds(pl.multiple_of(c * CHUNK, CHUNK), KEYS)
        scores, vals = [], []
        for s in range(SLOTS):
            cols = pl.ds(s * HD, HD)
            keys = jnp.concatenate([kc[0, window, cols], kc[1, window, cols]], axis=0)
            vals.append(jnp.concatenate([vc[0, window, cols], vc[1, window, cols]], axis=0))
            scores.append(lax.dot_general(
                qbuf[s], keys, (((1,), (1,)), ((), ())), preferred_element_type=jnp.float32
            ))
        weights = [jnp.where(allowed, jnp.exp(x * scale), 0.0) for x in scores]
        sums = [jnp.sum(x, axis=-1, keepdims=True) for x in weights]
        probs = [(x / y).astype(jnp.bfloat16) for x, y in zip(weights, sums)]
        attended = [
            jnp.dot(x, y, preferred_element_type=jnp.float32).astype(jnp.bfloat16)
            for x, y in zip(probs, vals)
        ]

        for turn in range(GROUP):
            cc = (cc_own + FAR[turn]) % GROUP
            total = None
            rows = pl.ds(pl.multiple_of(cc * PIECE, PIECE), PIECE)
            for s in (0, 2, 4):
                n = 2 if s < 4 else 1
                lhs = attended[s] if n == 1 else jnp.concatenate(attended[s : s + n], axis=1)
                rhs = [w[s + i, rows, pl.ds(3 * HD, HD)] for i in range(n)]
                rhs = rhs[0] if n == 1 else jnp.concatenate(rhs, axis=1)
                term = lax.dot_general(
                    lhs, rhs, (((1,), (1,)), ((), ())), preferred_element_type=jnp.float32
                )
                total = term if total is None else total + term
            cols = pl.ds(pl.multiple_of(cc * PIECE, PIECE), PIECE)
            if turn == 0:
                part[...] = total
            sendb[c, :, cols] = total.astype(jnp.bfloat16)
            for d in ((FAR[turn] + GROUP), FAR[turn]):
                if d > 0:
                    remote(
                        sendb.at[c, peer_rows[d], cols], rbuf.at[c, d - 1],
                        snd_r.at[c], sem_r.at[c], sec, peers[d],
                    ).start()

    def combine(c):
        total = part[row_own, :] + hbuf[c, row_own, col_own].astype(jnp.float32)
        drain(rbuf.at[c], sem_r.at[c])
        for d in range(DP - 1):
            total = total + rbuf[c, d].astype(jnp.float32)
        hnew[c] = total.astype(jnp.bfloat16)

        @pl.when(jnp.logical_not(last))
        def _():
            for n in (4, 3, 5, 2, 6, 1, 7, 0):
                remote(
                    hnew.at[c], hbuf.at[c, row_own, col_own],
                    snd_h.at[c], sem_h.at[c], next_sec, peers[n],
                ).start()

        @pl.when(last & (c < CHUNKS - 1))
        def _():
            to_sec = c * GROUP + cc_own
            remote(hnew.at[c], outb.at[:, col_own], snd_h.at[c], sem_o, to_sec, out_z).start()

        @pl.when(last & (c == CHUNKS - 1))
        def _():
            for n in range(GROUP):
                here = (n == g) & is_out

                @pl.when(here)
                def _():
                    pltpu.make_async_copy(hnew.at[c], outb.at[:, col_own], sem_o).start()

                @pl.when(jnp.logical_not(here))
                def _():
                    to_sec = sections - GROUP + n
                    remote(
                        hnew.at[c], outb.at[:, col_own], snd_h.at[c], sem_o, to_sec, out_z
                    ).start()

    def step(c, _):
        project(c)
        attend(c)
        combine(c)
        return 0

    lax.fori_loop(0, CHUNKS, step, 0)

    result = outb.at[:, pl.ds(pl.multiple_of(g * PIECE, PIECE), PIECE)]

    @pl.when(jnp.logical_not(last))
    def _():
        drain(result, sem_o)
        for to_sec in (c_mate, y_mate, base + GROUP - 1 - g):
            remote(result, result, snd_f, sem_f, to_sec, z).start()
        drain(outb.at[:, pl.ds(0, 3 * PIECE)], sem_f)
        drain(outb.at[:, pl.ds(0, 3 * PIECE)], snd_f)

    @pl.when(last)
    def _():
        drain(outb, sem_o)

    out_ref[...] = outb[...]

    def sent(c, _):
        drain(rbuf.at[c], snd_r.at[c])

        @pl.when(jnp.logical_not(last))
        def _():
            drain(hbuf.at[c], snd_h.at[c])

        @pl.when(last)
        def _():
            @pl.when(c < CHUNKS - 1)
            def _():
                drain(hnew.at[c], snd_h.at[c])

            @pl.when((c == CHUNKS - 1) & is_out)
            def _():
                drain(outb.at[:, pl.ds(0, 3 * PIECE)], snd_h.at[c])

            @pl.when((c == CHUNKS - 1) & jnp.logical_not(is_out))
            def _():
                drain(outb, snd_h.at[c])

        return 0

    lax.fori_loop(0, CHUNKS, sent, 0)

    def sent_weights(size):
        def one(d, _):
            drain(block(g, d, size), snd_y.at[d])
            drain(block(g, d, size), snd_c.at[d])
            drain(block(slot_y, d, size), snd_c2.at[d])

            @pl.when(takes & (size == ROWS))
            def _():
                drain(half(d, mine, size), snd_yx.at[d])
                drain(half(d, mine, size), snd_cx.at[d])
                drain(half(d, mine, size), snd_cx2.at[d])

            @pl.when(d > 0)
            def _():
                drain(block(g, 0, size), sem_w.at[d])

            return 0

        lax.fori_loop(0, DP, one, 0)
        if size == ROWS:
            for m in range(2):
                @pl.when(z != g + GROUP * m)
                def _():
                    drain(half(0, 0, size), sem_w.at[DP + m])

                drain(half(0, 0, size), sem_w.at[DP + 2 + m])
        else:
            for n in range(2):
                for r in range(4):
                    drain(staged.at[n, r], snd_s.at[0, n, r])
                    drain(extras.at[n, r], snd_s.at[1, n, r])

    @pl.when(early)
    def _():
        sent_weights(ROWS - GUEST)

    @pl.when(jnp.logical_not(early))
    def _():
        sent_weights(ROWS)

    @pl.when(helps)
    def _():
        for n in range(2):
            for r in range(4):
                drain(staged.at[n, r], snd_g.at[0, n, r])
                drain(extras.at[n, r], snd_g.at[1, n, r])

    @pl.when(feeds)
    def _():
        for n in range(2):
            drain(x_ref.at[0], snd_i.at[n])

    @pl.when(own_seq)
    def _():
        for d in range(1, DP):
            drain(span.at[2], snd_k.at[d - 1])


def shards(inputs, span_lengths, qkv_weight, out_weight):
    sections = lax.axis_size("section")
    bf16 = jnp.bfloat16
    dma = lambda *n: pltpu.SemaphoreType.DMA(n)
    out = pl.pallas_call(
        kernel,
        out_shape=jax.ShapeDtypeStruct((CHUNK, WIDTH), bf16),
        in_specs=[
            pl.BlockSpec(memory_space=pl.ANY),
            pl.BlockSpec(memory_space=pltpu.VMEM),
            pl.BlockSpec(memory_space=pl.ANY),
            pl.BlockSpec(memory_space=pl.ANY),
        ],
        out_specs=pl.BlockSpec(memory_space=pltpu.VMEM),
        scratch_shapes=[
            pltpu.VMEM((SLOTS, WIDTH, 4 * HD), bf16),
            pltpu.VMEM((CHUNKS, 2 * CHUNK, WIDTH), bf16),
            pltpu.VMEM((2 * CHUNK, WIDTH), bf16),
            pltpu.VMEM((SLOTS, 2 * CHUNK, HD), bf16),
            pltpu.VMEM((2, LEN + BACK, SLOTS * HD), bf16),
            pltpu.VMEM((2, LEN + BACK, SLOTS * HD), bf16),
            pltpu.VMEM((3, 8, HD), jnp.int32),
            pltpu.VMEM((2, LEN, HD), jnp.float32),
            pltpu.VMEM((CHUNKS, 2 * CHUNK, 2 * KEYS), jnp.float32),
            pltpu.VMEM((2 * CHUNK, PIECE), jnp.float32),
            pltpu.VMEM((CHUNKS, 2 * CHUNK, WIDTH), bf16),
            pltpu.VMEM((CHUNKS, DP - 1, CHUNK, PIECE), bf16),
            pltpu.VMEM((CHUNKS, CHUNK, PIECE), bf16),
            pltpu.VMEM((CHUNK, WIDTH), bf16),
            pltpu.VMEM((2, 4, GUEST, DP * HD), bf16),
            pltpu.VMEM((2, 4, ROWS, 2 * HD), bf16),
            dma(2, 2, 4), dma(2, 2, 4), dma(2, 2, 4), dma(DP), dma(DP), dma(DP),
            dma(DP + 4), dma(DP), dma(DP), dma(DP), dma(DP), dma(DP), dma(DP), dma(DP),
            dma(DP), dma(DP), dma(DP), dma(DP), dma(DP), dma(DP),
            pltpu.SemaphoreType.DMA, dma(DP - 1), dma(CHUNKS), dma(CHUNKS), dma(CHUNKS),
            dma(CHUNKS), dma(CHUNKS), pltpu.SemaphoreType.DMA, pltpu.SemaphoreType.DMA,
            pltpu.SemaphoreType.DMA,
        ],
        compiler_params=pltpu.CompilerParams(
            collective_id=0, has_side_effects=True, vmem_limit_bytes=60 * 1024 * 1024
        ),
    )(inputs, span_lengths, qkv_weight, out_weight)
    rows = LEN // sections
    first = lax.axis_index("section") % (CHUNK // rows) * rows
    return lax.dynamic_slice(out, (first, 0), (rows, WIDTH))[None]


def solution(mesh):
    in_specs = (
        P("dp", None, None),
        P("dp", None),
        P("section", "dp", None),
        P("section", "dp", None),
    )
    out_specs = P("dp", "section", None)
    return jax.shard_map(shards, mesh=mesh, in_specs=in_specs, out_specs=out_specs, check_vma=False)
```

```python
import jax
import jax.numpy as jnp
from jax import lax
from jax.experimental import pallas as pl
from jax.experimental.pallas import tpu as pltpu
from jax.sharding import PartitionSpec as P

HD = 128
GROUP = 4
SPANS = 8
LEN = 128
DP = 8
WIDTH = 2560
ROWS = 320
SLOTS = 5
CHUNK = 16
CHUNKS = LEN // CHUNK
BACK = 48
KEYS = BACK + CHUNK
PIECE = 640
AHEAD = 3
FAR = (0, 3, 1, 2)
EARLY = 2
GUEST = 16
MESH = pl.DeviceIdType.MESH


def kernel(
    x_ref, sp_ref, qkv_ref, ow_ref, out_ref,
    w, hbuf, normed, qbuf, kc, vc, span, first_ref, mask_ref, part, sendb, rbuf, hnew, outb,
    staged, extras, sem_s, snd_s, snd_g, sem_gz, sem_gc, snd_gc,
    sem_w, sem_z, sem_x, sem_y, sem_yx, sem_c, sem_c2, sem_cx,
    snd_y, snd_yx, snd_c, snd_c2, snd_cx, snd_cx2,
    sem_k, snd_k, sem_h, snd_i, sem_r, snd_r, snd_h, sem_o, sem_f, snd_f,
):
    sec = lax.axis_index("section")
    z = lax.axis_index("dp")
    sections = lax.axis_size("section")
    layers = sections // GROUP
    layer = sec // GROUP
    last = layer == layers - 1
    g = sec % GROUP
    base = layer * GROUP
    slot_y = (g + 2) % GROUP
    y_mate = base + slot_y
    mate = g + 1 - 2 * (g % 2)
    c_mate = base + mate
    slot_cy = (mate + 2) % GROUP
    zg = z % GROUP

    q = (g + 2 * (layer % 2)) % GROUP
    q_z = (z % 2) * 2 + z % GROUP // 2
    e_z = z // GROUP
    own_seq = q_z == q
    feeds = (layer >= layers // 2) & (q_z == g)
    e_own = z // GROUP
    cc_own = z % GROUP
    out_z = GROUP * e_own + 2 * (q % 2) + q // 2
    is_out = out_z == z
    next_sec = base + GROUP + slot_y
    peers = [(z + d) % DP for d in range(DP)]
    peer_rows = [pl.ds(pl.multiple_of(p // GROUP * CHUNK, CHUNK), CHUNK) for p in peers]

    early = layer < EARLY
    helps = layer >= layers - EARLY
    shift = (layers - EARLY) * GROUP

    def remote(src, dst, s_sem, r_sem, to_sec, to_z):
        return pltpu.make_async_remote_copy(
            src_ref=src, dst_ref=dst, send_sem=s_sem, recv_sem=r_sem,
            device_id=(to_sec, to_z), device_id_type=MESH,
        )

    def drain(ref, sem):
        pltpu.make_async_copy(ref, ref, sem).wait()

    barrier = pltpu.get_barrier_semaphore()

    def greet(to_sec, to_z):
        pl.semaphore_signal(barrier, inc=1, device_id=(to_sec, to_z), device_id_type=MESH)

    for d in range(1, DP):
        greet(sec, (z + d) % DP)
    greet(y_mate, z)
    greet(c_mate, z)
    for d in range(1, DP):
        greet(y_mate, (z + d) % DP)

    @pl.when(layer > 0)
    def _():
        for d in range(DP):
            greet(base - GROUP + slot_y, (z + d) % DP)

    @pl.when(early)
    def _():
        for d in range(DP):
            greet(sec + shift, (z + d) % DP)

    @pl.when(helps)
    def _():
        greet(sec - shift, z)
        greet(y_mate - shift, z)

    @pl.when(layer == 0)
    def _():
        for n in range(layers // 2):
            for e in range(2):
                greet((layers // 2 + n) * GROUP + g, 4 * e + 2 * (g % 2) + g // 2)

    g_out = (q_z + 2 * ((layers - 1) % 2)) % GROUP
    from_sec = sections - GROUP + g_out

    @pl.when(jnp.logical_not(last))
    def _():
        greet(base + GROUP - 1 - g, z)
        greet(from_sec, e_z * GROUP + g)

    @pl.when(last)
    def _():
        for cc in range(GROUP):
            from_z = e_z * GROUP + cc

            @pl.when((from_sec != sec) | (from_z != z))
            def _():
                greet(from_sec, from_z)

    kc[:, pl.ds(0, BACK), :] = jnp.zeros((2, BACK, SLOTS * HD), jnp.bfloat16)
    vc[:, pl.ds(0, BACK), :] = jnp.zeros((2, BACK, SLOTS * HD), jnp.bfloat16)
    span[2] = jnp.zeros((8, HD), jnp.int32)
    span[2, pl.ds(0, 1), pl.ds(0, SPANS)] = sp_ref[...]

    partners = 2 * DP + jnp.where(last, layers - 1 + GROUP - is_out.astype(jnp.int32), DP + 1)
    partners += DP * feeds.astype(jnp.int32) + 2 * early.astype(jnp.int32)
    pl.semaphore_wait(barrier, partners + DP * helps.astype(jnp.int32))

    @pl.when(own_seq)
    def _():
        pltpu.make_async_copy(span.at[2], span.at[e_z], sem_k).start()
        for d in range(1, DP):
            remote(span.at[2], span.at[e_z], snd_k.at[d - 1], sem_k, sec, (z + d) % DP).start()

    def feed(c):
        src = x_ref.at[0, pl.ds(pl.multiple_of(c * CHUNK, CHUNK), CHUNK), :]
        dst = hbuf.at[c, pl.ds(pl.multiple_of(e_z * CHUNK, CHUNK), CHUNK), :]
        for d in range(DP):
            remote(src, dst, snd_i.at[c % 2], sem_h.at[c], g, (z + d) % DP).start()

    @pl.when(feeds)
    def _():
        for n in range(2):
            feed(2 * (layer - layers // 2) + n)

    def hand_over():
        for r in range(4):
            for kind in range(2):
                rows = pl.ds(ROWS - GUEST, GUEST) if kind == 0 else pl.ds(0, ROWS)
                first, count = (0, DP * HD) if kind == 0 else (DP * HD, 2 * HD)
                if r < 3:
                    src = qkv_ref.at[0, rows, pl.ds(10 * HD * r + first, count)]
                else:
                    src = ow_ref.at[0, rows, pl.ds(first, count)]
                for n, to_sec in enumerate((sec, y_mate)):
                    dst = (staged if kind == 0 else extras).at[n, r]
                    remote(
                        src, dst, snd_s.at[kind, n, r], sem_s.at[kind, n, r], to_sec + shift, z
                    ).start()

    def pass_on(r, _):
        some = pl.ds(pl.multiple_of(z * ROWS + ROWS - GUEST, 16), GUEST)
        every = pl.ds(pl.multiple_of(z * ROWS, 16), ROWS)
        cols = pl.ds(pl.multiple_of(r * HD, HD), HD)
        for n, slot in enumerate((g, slot_y)):
            drain(staged.at[n, r], sem_s.at[0, n, r])
            for j in (4, 3, 5, 2, 6, 1, 7, 0):
                to_z = (z + j) % DP
                src = staged.at[n, r, :, pl.ds(pl.multiple_of(to_z * HD, HD), HD)]
                remote(
                    src, w.at[slot, some, cols], snd_g.at[0, n, r], sem_gz.at[z],
                    sec - shift, to_z,
                ).start()
        for n, slot in enumerate((g, slot_y)):
            drain(extras.at[n, r], sem_s.at[1, n, r])
            for m in range(2):
                src = extras.at[n, r, :, pl.ds(m * HD, HD)]
                remote(
                    src, w.at[4, every, cols], snd_g.at[1, n, r], sem_gz.at[z],
                    sec - shift, slot + GROUP * m,
                ).start()
        return 0

    def take_guests(n, _):
        z_s = (z + DP - order(n)) % DP
        rows = pl.ds(pl.multiple_of(z_s * ROWS + ROWS - GUEST, 16), GUEST)

        @pl.when(takes)
        def _():
            drain(w.at[0, pl.ds(0, 2 * GUEST + ROWS), :], sem_gz.at[z_s])
            x = block(4, order(n), ROWS)
            remote(x, x, snd_gc.at[z_s], sem_gc.at[z_s], c_mate, z).start()

        @pl.when(jnp.logical_not(takes))
        def _():
            drain(w.at[0, pl.ds(0, 2 * GUEST), :], sem_gz.at[z_s])

        for slot in (g, slot_y):
            x = w.at[slot, rows, :]
            remote(x, x, snd_gc.at[z_s], sem_gc.at[z_s], c_mate, z).start()
        return 0

    def settle_guests(z_s, _):
        @pl.when(takes)
        def _():
            drain(w.at[0, pl.ds(0, 2 * GUEST), :], sem_gc.at[z_s])
            drain(w.at[0, pl.ds(0, 2 * GUEST + ROWS), :], snd_gc.at[z_s])

        @pl.when(jnp.logical_not(takes))
        def _():
            drain(w.at[0, pl.ds(0, 2 * GUEST + ROWS), :], sem_gc.at[z_s])
            drain(w.at[0, pl.ds(0, 2 * GUEST), :], snd_gc.at[z_s])

        return 0

    takes = (zg == g) | (zg == slot_y)
    mine = jnp.where(zg == g, 0, 2 * HD)

    def order(n):
        return ((1 - 2 * (n % 2)) * ((n + 1) // 2) + DP) % DP

    def block(slot, d, size):
        return w.at[slot, pl.ds(pl.multiple_of((z + DP - d) % DP * ROWS, ROWS), size), :]

    def half(d, at, size):
        rows = pl.ds(pl.multiple_of((z + DP - d) % DP * ROWS, ROWS), size)
        return w.at[4, rows, pl.ds(pl.multiple_of(at, 2 * HD), 2 * HD)]

    def prepare():
        drain(span.at[pl.ds(0, 2)], sem_k)
        lane = lax.broadcasted_iota(jnp.int32, (1, HD), 1)
        token = lax.broadcasted_iota(jnp.int32, (LEN, HD), 0).astype(jnp.float32)
        for e in range(2):
            lens = span[e, pl.ds(0, 1), :].astype(jnp.float32)
            key_start = jnp.zeros((LEN, HD), jnp.float32)
            before = jnp.zeros((1, 1), jnp.float32)
            for s in range(1, SPANS):
                start = jnp.sum(jnp.where(lane < s, lens, 0.0), axis=1, keepdims=True)
                key_start = jnp.where(token >= start, before, key_start)
                before = start
            first_ref[e] = key_start

        def mask(c, _):
            tok = pl.ds(pl.multiple_of(c * CHUNK, CHUNK), CHUNK)
            first = jnp.concatenate([first_ref[0, tok, :], first_ref[1, tok, :]], axis=0)
            row = lax.broadcasted_iota(jnp.int32, (2 * CHUNK, 2 * KEYS), 0)
            col = lax.broadcasted_iota(jnp.int32, (2 * CHUNK, 2 * KEYS), 1)
            same = (row < CHUNK) == (col < KEYS)
            key_pos = c * CHUNK - BACK + jnp.where(col < KEYS, col, col - KEYS)
            tok_pos = c * CHUNK + jnp.where(row < CHUNK, row, row - CHUNK)
            allowed = same & (key_pos <= tok_pos) & (key_pos.astype(jnp.float32) >= first)
            mask_ref[c] = allowed.astype(jnp.float32)
            return 0

        lax.fori_loop(0, CHUNKS, mask, 0)

    def relayout(size):
        def parts(i, slot):
            rows = pl.ds(pl.multiple_of(z * ROWS, ROWS), size)
            col = lambda n: pl.ds(pl.multiple_of(n * HD, HD), HD)
            out = []
            for p in range(3):
                out.append((qkv_ref.at[0, pl.ds(0, size), col(10 * p + i)], w.at[slot, rows, pl.ds(HD * p, HD)]))
            out.append((ow_ref.at[0, pl.ds(0, size), col(i)], w.at[slot, rows, pl.ds(3 * HD, HD)]))
            return out

        def send_round(n):
            d = order(n)
            to_z = (z + d) % DP
            head = parts(to_z, g)

            @pl.when(to_z == z)
            def _():
                for src, dst in head:
                    pltpu.make_async_copy(src, dst, sem_z.at[0]).start()

            @pl.when(to_z != z)
            def _():
                for src, dst in head:
                    remote(src, dst, sem_w.at[n], sem_z.at[d], sec, to_z).start()

            @pl.when((to_z % GROUP == g) & (size == ROWS))
            def _():
                m = to_z // GROUP
                extra = parts(8 + m, 4)

                @pl.when(to_z == z)
                def _():
                    for src, dst in extra[:2]:
                        pltpu.make_async_copy(src, dst, sem_x.at[0]).start()

                @pl.when(to_z != z)
                def _():
                    for src, dst in extra[:2]:
                        remote(src, dst, sem_w.at[DP + m], sem_x.at[d], sec, to_z).start()

                for src, dst in extra[2:]:
                    remote(src, dst, sem_w.at[DP + 2 + m], sem_x.at[d], y_mate, to_z).start()

        ahead = 4 if size < ROWS else AHEAD
        for n in range(ahead):
            send_round(n)
        if size < ROWS:
            hand_over()

        def relay(n, _):
            @pl.when(n < DP)
            def _():
                d = order(n)
                b = block(g, d, size)
                drain(b, sem_z.at[d])
                remote(b, b, snd_y.at[d], sem_y.at[d], y_mate, z).start()
                remote(b, b, snd_c.at[d], sem_c.at[d], c_mate, z).start()

                @pl.when(takes & (size == ROWS))
                def _():
                    x = half(d, mine, size)
                    drain(x, sem_x.at[d])
                    remote(x, x, snd_yx.at[d], sem_yx.at[d], y_mate, z).start()
                    remote(x, x, snd_cx.at[d], sem_cx.at[d], c_mate, z).start()

            @pl.when(n + ahead < DP)
            def _():
                send_round(n + ahead)

            @pl.when(n > 0)
            def _():
                d = order(n - 1)
                b = block(slot_y, d, size)
                drain(b, sem_y.at[d])
                remote(b, b, snd_c2.at[d], sem_c2.at[d], c_mate, z).start()

                @pl.when(takes & (size == ROWS))
                def _():
                    x = half(d, 2 * HD - mine, size)
                    drain(x, sem_yx.at[d])
                    remote(x, x, snd_cx2.at[d], sem_cx.at[d], c_mate, z).start()

            return 0

        lax.fori_loop(0, DP + 1, relay, 0)
        prepare()
        if size < ROWS:
            lax.fori_loop(0, DP, take_guests, 0)

        def arrive(n, _):
            d = order(n)
            drain(block(mate, d, size), sem_c.at[d])
            drain(block(slot_cy, d, size), sem_c2.at[d])

            @pl.when(jnp.logical_not(takes) & (size == ROWS))
            def _():
                drain(block(4, d, size), sem_cx.at[d])

            return 0

        lax.fori_loop(0, DP, arrive, 0)

        if size < ROWS:
            lax.fori_loop(0, DP, settle_guests, 0)

    @pl.when(helps)
    def _():
        lax.fori_loop(0, 4, pass_on, 0)

    @pl.when(early)
    def _():
        relayout(ROWS - GUEST)

    @pl.when(jnp.logical_not(early))
    def _():
        relayout(ROWS)

    row_own = pl.ds(pl.multiple_of(e_own * CHUNK, CHUNK), CHUNK)
    col_own = pl.ds(pl.multiple_of(cc_own * PIECE, PIECE), PIECE)
    scale = HD ** (-0.5)

    def project(c):
        drain(hbuf.at[c], sem_h.at[c])
        values = hbuf[c].astype(jnp.float32)
        mean = jnp.mean(values, axis=-1, keepdims=True)
        centred = values - mean
        var = jnp.mean(centred * centred, axis=-1, keepdims=True)
        normed[...] = (centred * lax.rsqrt(var + 1e-05)).astype(jnp.bfloat16)

        def columns(cols):
            mat = [w[s, :, pl.ds(p * HD, HD * n)] for s, p, n in cols]
            mat = mat[0] if len(mat) == 1 else jnp.concatenate(mat, axis=1)
            return jnp.dot(normed[...], mat, preferred_element_type=jnp.float32).astype(jnp.bfloat16)

        new = pl.ds(pl.multiple_of(c * CHUNK + BACK, CHUNK), CHUNK)
        for s in range(SLOTS):
            qk = columns([(s, 0, 2)])
            qbuf[s] = qk[:, :HD]
            kc[0, new, pl.ds(s * HD, HD)] = qk[:CHUNK, HD:]
            kc[1, new, pl.ds(s * HD, HD)] = qk[CHUNK:, HD:]
        for s in (0, 2, 4):
            n = 2 if s < 4 else 1
            v = columns([(s + i, 2, 1) for i in range(n)])
            vc[0, new, pl.ds(s * HD, n * HD)] = v[:CHUNK]
            vc[1, new, pl.ds(s * HD, n * HD)] = v[CHUNK:]

    def attend(c):
        allowed = mask_ref[c] > 0.0
        window = pl.ds(pl.multiple_of(c * CHUNK, CHUNK), KEYS)
        scores, vals = [], []
        for s in range(SLOTS):
            cols = pl.ds(s * HD, HD)
            keys = jnp.concatenate([kc[0, window, cols], kc[1, window, cols]], axis=0)
            vals.append(jnp.concatenate([vc[0, window, cols], vc[1, window, cols]], axis=0))
            scores.append(lax.dot_general(
                qbuf[s], keys, (((1,), (1,)), ((), ())), preferred_element_type=jnp.float32
            ))
        weights = [jnp.where(allowed, jnp.exp(x * scale), 0.0) for x in scores]
        sums = [jnp.sum(x, axis=-1, keepdims=True) for x in weights]
        probs = [(x / y).astype(jnp.bfloat16) for x, y in zip(weights, sums)]
        attended = [
            jnp.dot(x, y, preferred_element_type=jnp.float32).astype(jnp.bfloat16)
            for x, y in zip(probs, vals)
        ]

        for turn in range(GROUP):
            cc = (cc_own + FAR[turn]) % GROUP
            total = None
            rows = pl.ds(pl.multiple_of(cc * PIECE, PIECE), PIECE)
            for s in (0, 2, 4):
                n = 2 if s < 4 else 1
                lhs = attended[s] if n == 1 else jnp.concatenate(attended[s : s + n], axis=1)
                rhs = [w[s + i, rows, pl.ds(3 * HD, HD)] for i in range(n)]
                rhs = rhs[0] if n == 1 else jnp.concatenate(rhs, axis=1)
                term = lax.dot_general(
                    lhs, rhs, (((1,), (1,)), ((), ())), preferred_element_type=jnp.float32
                )
                total = term if total is None else total + term
            cols = pl.ds(pl.multiple_of(cc * PIECE, PIECE), PIECE)
            if turn == 0:
                part[...] = total
            sendb[c, :, cols] = total.astype(jnp.bfloat16)
            for d in ((FAR[turn] + GROUP), FAR[turn]):
                if d > 0:
                    remote(
                        sendb.at[c, peer_rows[d], cols], rbuf.at[c, d - 1],
                        snd_r.at[c], sem_r.at[c], sec, peers[d],
                    ).start()

    def combine(c):
        total = part[row_own, :] + hbuf[c, row_own, col_own].astype(jnp.float32)
        drain(rbuf.at[c], sem_r.at[c])
        for d in range(DP - 1):
            total = total + rbuf[c, d].astype(jnp.float32)
        hnew[c] = total.astype(jnp.bfloat16)

        @pl.when(jnp.logical_not(last))
        def _():
            for n in (4, 3, 5, 2, 6, 1, 7, 0):
                remote(
                    hnew.at[c], hbuf.at[c, row_own, col_own],
                    snd_h.at[c], sem_h.at[c], next_sec, peers[n],
                ).start()

        @pl.when(last & (c < CHUNKS - 1))
        def _():
            to_sec = c * GROUP + cc_own
            remote(hnew.at[c], outb.at[:, col_own], snd_h.at[c], sem_o, to_sec, out_z).start()

        @pl.when(last & (c == CHUNKS - 1))
        def _():
            for n in range(GROUP):
                here = (n == g) & is_out

                @pl.when(here)
                def _():
                    pltpu.make_async_copy(hnew.at[c], outb.at[:, col_own], sem_o).start()

                @pl.when(jnp.logical_not(here))
                def _():
                    to_sec = sections - GROUP + n
                    remote(
                        hnew.at[c], outb.at[:, col_own], snd_h.at[c], sem_o, to_sec, out_z
                    ).start()

    def step(c, _):
        project(c)
        attend(c)
        combine(c)
        return 0

    lax.fori_loop(0, CHUNKS, step, 0)

    result = outb.at[:, pl.ds(pl.multiple_of(g * PIECE, PIECE), PIECE)]

    @pl.when(jnp.logical_not(last))
    def _():
        drain(result, sem_o)
        for to_sec in (c_mate, y_mate, base + GROUP - 1 - g):
            remote(result, result, snd_f, sem_f, to_sec, z).start()
        drain(outb.at[:, pl.ds(0, 3 * PIECE)], sem_f)
        drain(outb.at[:, pl.ds(0, 3 * PIECE)], snd_f)

    @pl.when(last)
    def _():
        drain(outb, sem_o)

    out_ref[...] = outb[...]

    def sent(c, _):
        drain(rbuf.at[c], snd_r.at[c])

        @pl.when(jnp.logical_not(last))
        def _():
            drain(hbuf.at[c], snd_h.at[c])

        @pl.when(last)
        def _():
            @pl.when(c < CHUNKS - 1)
            def _():
                drain(hnew.at[c], snd_h.at[c])

            @pl.when((c == CHUNKS - 1) & is_out)
            def _():
                drain(outb.at[:, pl.ds(0, 3 * PIECE)], snd_h.at[c])

            @pl.when((c == CHUNKS - 1) & jnp.logical_not(is_out))
            def _():
                drain(outb, snd_h.at[c])

        return 0

    lax.fori_loop(0, CHUNKS, sent, 0)

    def sent_weights(size):
        def one(d, _):
            drain(block(g, d, size), snd_y.at[d])
            drain(block(g, d, size), snd_c.at[d])
            drain(block(slot_y, d, size), snd_c2.at[d])

            @pl.when(takes & (size == ROWS))
            def _():
                drain(half(d, mine, size), snd_yx.at[d])
                drain(half(d, mine, size), snd_cx.at[d])
                drain(half(d, mine, size), snd_cx2.at[d])

            @pl.when(d > 0)
            def _():
                drain(block(g, 0, size), sem_w.at[d])

            return 0

        lax.fori_loop(0, DP, one, 0)
        if size == ROWS:
            for m in range(2):
                @pl.when(z != g + GROUP * m)
                def _():
                    drain(half(0, 0, size), sem_w.at[DP + m])

                drain(half(0, 0, size), sem_w.at[DP + 2 + m])
        else:
            for n in range(2):
                for r in range(4):
                    drain(staged.at[n, r], snd_s.at[0, n, r])
                    drain(extras.at[n, r], snd_s.at[1, n, r])

    @pl.when(early)
    def _():
        sent_weights(ROWS - GUEST)

    @pl.when(jnp.logical_not(early))
    def _():
        sent_weights(ROWS)

    @pl.when(helps)
    def _():
        for n in range(2):
            for r in range(4):
                drain(staged.at[n, r], snd_g.at[0, n, r])
                drain(extras.at[n, r], snd_g.at[1, n, r])

    @pl.when(feeds)
    def _():
        for n in range(2):
            drain(x_ref.at[0], snd_i.at[n])

    @pl.when(own_seq)
    def _():
        for d in range(1, DP):
            drain(span.at[2], snd_k.at[d - 1])


def shards(inputs, span_lengths, qkv_weight, out_weight):
    sections = lax.axis_size("section")
    bf16 = jnp.bfloat16
    dma = lambda *n: pltpu.SemaphoreType.DMA(n)
    out = pl.pallas_call(
        kernel,
        out_shape=jax.ShapeDtypeStruct((CHUNK, WIDTH), bf16),
        in_specs=[
            pl.BlockSpec(memory_space=pl.ANY),
            pl.BlockSpec(memory_space=pltpu.VMEM),
            pl.BlockSpec(memory_space=pl.ANY),
            pl.BlockSpec(memory_space=pl.ANY),
        ],
        out_specs=pl.BlockSpec(memory_space=pltpu.VMEM),
        scratch_shapes=[
            pltpu.VMEM((SLOTS, WIDTH, 4 * HD), bf16),
            pltpu.VMEM((CHUNKS, 2 * CHUNK, WIDTH), bf16),
            pltpu.VMEM((2 * CHUNK, WIDTH), bf16),
            pltpu.VMEM((SLOTS, 2 * CHUNK, HD), bf16),
            pltpu.VMEM((2, LEN + BACK, SLOTS * HD), bf16),
            pltpu.VMEM((2, LEN + BACK, SLOTS * HD), bf16),
            pltpu.VMEM((3, 8, HD), jnp.int32),
            pltpu.VMEM((2, LEN, HD), jnp.float32),
            pltpu.VMEM((CHUNKS, 2 * CHUNK, 2 * KEYS), jnp.float32),
            pltpu.VMEM((2 * CHUNK, PIECE), jnp.float32),
            pltpu.VMEM((CHUNKS, 2 * CHUNK, WIDTH), bf16),
            pltpu.VMEM((CHUNKS, DP - 1, CHUNK, PIECE), bf16),
            pltpu.VMEM((CHUNKS, CHUNK, PIECE), bf16),
            pltpu.VMEM((CHUNK, WIDTH), bf16),
            pltpu.VMEM((2, 4, GUEST, DP * HD), bf16),
            pltpu.VMEM((2, 4, ROWS, 2 * HD), bf16),
            dma(2, 2, 4), dma(2, 2, 4), dma(2, 2, 4), dma(DP), dma(DP), dma(DP),
            dma(DP + 4), dma(DP), dma(DP), dma(DP), dma(DP), dma(DP), dma(DP), dma(DP),
            dma(DP), dma(DP), dma(DP), dma(DP), dma(DP), dma(DP),
            pltpu.SemaphoreType.DMA, dma(DP - 1), dma(CHUNKS), dma(CHUNKS), dma(CHUNKS),
            dma(CHUNKS), dma(CHUNKS), pltpu.SemaphoreType.DMA, pltpu.SemaphoreType.DMA,
            pltpu.SemaphoreType.DMA,
        ],
        compiler_params=pltpu.CompilerParams(
            collective_id=0, has_side_effects=True, vmem_limit_bytes=60 * 1024 * 1024
        ),
    )(inputs, span_lengths, qkv_weight, out_weight)
    rows = LEN // sections
    first = lax.axis_index("section") % (CHUNK // rows) * rows
    return lax.dynamic_slice(out, (first, 0), (rows, WIDTH))[None]


def solution(mesh):
    in_specs = (
        P("dp", None, None),
        P("dp", None),
        P("section", "dp", None),
        P("section", "dp", None),
    )
    out_specs = P("dp", "section", None)
    return jax.shard_map(shards, mesh=mesh, in_specs=in_specs, out_specs=out_specs, check_vma=False)
```
